512 devices in a mesh: seq: 16 (over x, z_hi), res: 32 (over y, z_lo, core).
Axes of the slice: x: 4, y: 4, z: 16 (z_hi: 4, z_lo: 4; z = z_hi * 4 + z_lo), core: 2. Of those that a mesh axis runs over, the one named last changes fastest.
Arguments:
- alignment: bfloat16 [32, 2048, 256], P('seq', 'res'), may hold values from -6 to 6
- align_mask: int32 [32, 2048], P('seq', 'res'), may hold values from 0 to 1
- residue_mask: int32 [2048], P('res'), may hold values 0 or 1
- left_weight: bfloat16 [256, 32], replicated, may hold values from -0.375 to 0.375
- right_weight: bfloat16 [256, 32], replicated, may hold values from -0.375 to 0.375
- out_weight: bfloat16 [1024, 128], replicated, may hold values from -0.625 to 0.625
- pair_cotangent: bfloat16 [2048, 32, 64, 128], P('res', None, 'seq'), may hold values from -6 to 6
Outputs:
- pair_update: bfloat16 [2048, 32, 64, 128], P('res', None, 'seq')
- alignment_grad: bfloat16 [32, 2048, 256], P('seq', 'res')
- out_weight_grad: float32 [1024, 128], replicated
The draws below stay inside these ranges and needn't reach their ends.
All inputs are finite; a program needn't handle non-finite values. No bound on the sum of `residue_mask` on one device may be relied on, other than what follows from the above.
Results may differ from the reference program's by a relative error of at most 0.008.
Values may be sent and summed in bfloat16 or wider, within the bound.
A program may use at most 64 MiB of HBM per device.

```python
import jax
import jax.numpy as jnp
from jax import lax

CM = 256
C = 32
PAIR = 128
RES_DEV = 64
SEQS = 32
R = 2048


def draw_align_mask(key, part):
    key = jax.random.fold_in(key, 11)
    rolls = jax.random.randint(key, (SEQS, R), 0, 100)
    rank = jnp.arange(SEQS, dtype=jnp.int32)[:, None]
    keep = 95 - 60 * rank // SEQS
    return (rolls < keep).astype(jnp.int32)


def with_ends(values, stream_key, least, largest):
    dims = values.shape
    place = [jax.random.randint(jax.random.fold_in(stream_key, axis), (), 0, dims[axis]) for axis in range(len(dims))]
    values = values.at[tuple(place)].set(least)
    longest = dims.index(max(dims))
    place[longest] = (place[longest] + 1) % dims[longest]
    return values.at[tuple(place)].set(largest)


def levels(own_key, extent, pieces, least, high):
    factor_of = 1.0
    for position, parts in pieces:
        steps = jax.random.uniform(jax.random.fold_in(jax.random.fold_in(own_key, 6), position), (parts,), jnp.float32, least / len(pieces), high / len(pieces))
        factor_of = factor_of * jnp.repeat(jnp.exp(steps), extent[position] // parts).reshape((-1,) + (1,) * (len(extent) - 1 - position))
    return factor_of


def normal_values(stream_key, extent, scale, bound, cuts=(), kind=jnp.bfloat16):
    entries = jax.random.normal(stream_key, extent, jnp.float32) * scale
    if len(cuts) > 0:
        entries = levels(stream_key, extent, cuts, -0.22, 0.18) * entries
    return jnp.clip(entries, min=-bound, max=bound).astype(kind)


def setup_inputs(seed: int = 0) -> dict:
    splits = jax.random.split(jax.random.key(seed), 8)
    alignment = normal_values(splits[0], (SEQS, R, CM), 1.0, 6.0, ((0, 16), (1, 32)))
    align_mask = draw_align_mask(jax.random.fold_in(splits[7], 71), 0)
    residue_mask = with_ends((jax.random.randint(splits[2], (R,), 0, 16) < 15).astype(jnp.int32), jax.random.fold_in(splits[2], 1), 0, 1)
    left_weight = normal_values(splits[3], (CM, C), CM ** -0.5, 0.375)
    right_weight = normal_values(splits[4], (CM, C), CM ** -0.5, 0.375)
    out_weight = normal_values(splits[5], (C * C, PAIR), (max(1, 2560 // SEQS)) ** -0.5, 0.625)
    pair_cotangent = normal_values(splits[6], (R, R // RES_DEV, RES_DEV, PAIR), 1.0, 6.0, ((0, 32), (2, 16)))
    return {"alignment": alignment, "align_mask": align_mask, "residue_mask": residue_mask, "left_weight": left_weight, "right_weight": right_weight, "out_weight": out_weight, "pair_cotangent": pair_cotangent}


def project_rows(alignment, align_mask, residue_mask, left_weight, right_weight):
    values = alignment.astype(jnp.float32)
    center = values - lax.optimization_barrier(jnp.mean(values, -1, keepdims=True))
    inverse = lax.rsqrt(lax.optimization_barrier(jnp.mean(center * center, -1, keepdims=True)) + 1e-05)
    normal_rows = center * inverse
    rounded = normal_rows.astype(jnp.bfloat16)
    weights = (align_mask * residue_mask[None, :]).astype(jnp.float32)
    left_rows = (weights[..., None] * jnp.dot(rounded, left_weight, preferred_element_type=jnp.float32)).astype(jnp.bfloat16)
    right_rows = (weights[..., None] * jnp.dot(rounded, right_weight, preferred_element_type=jnp.float32)).astype(jnp.bfloat16)
    return (normal_rows, inverse, weights, left_rows, right_rows)

def norm_backward(normal_rows, inverse, weights, left_grad, right_grad, left_weight, right_weight):
    norm_grad = jnp.dot(weights[..., None] * left_grad, left_weight.astype(jnp.float32).T, precision=lax.Precision.HIGHEST)
    norm_grad = norm_grad + jnp.dot(weights[..., None] * right_grad, right_weight.astype(jnp.float32).T, precision=lax.Precision.HIGHEST)
    first = lax.optimization_barrier(jnp.mean(norm_grad, -1, keepdims=True))
    second = lax.optimization_barrier(jnp.mean(norm_grad * normal_rows, -1, keepdims=True))
    return (inverse * (norm_grad - first - normal_rows * second)).astype(jnp.bfloat16)

def reference(alignment, align_mask, residue_mask, left_weight, right_weight, out_weight, pair_cotangent):
    normal_rows, inverse, weights, left_rows, right_rows = project_rows(alignment, align_mask, residue_mask, left_weight, right_weight)
    counts = jnp.dot(weights.T, weights, precision=lax.Precision.HIGHEST)
    denom = jnp.maximum(counts, 1.0)
    cotangent = pair_cotangent.reshape(R, R, PAIR)
    left_full = left_rows.astype(jnp.float32)
    right_full = right_rows.astype(jnp.float32)
    block = 32

    def step(carry, start):
        weight_grad, right_grad = carry
        left_block = lax.dynamic_slice_in_dim(left_full, start, block, 1)
        outer = jnp.einsum('sic,sjd->ijcd', left_block, right_full).reshape(block * R, C * C).astype(jnp.bfloat16)
        scale_rows = lax.dynamic_slice_in_dim(denom, start, block, 0).reshape(block * R, 1)
        pair = (jnp.dot(outer, out_weight, preferred_element_type=jnp.float32) / scale_rows).astype(jnp.bfloat16)
        incoming = lax.dynamic_slice_in_dim(cotangent, start, block, 0).reshape(block * R, PAIR)
        scaled = (incoming.astype(jnp.float32) / scale_rows).astype(jnp.bfloat16)
        weight_grad = weight_grad + jnp.dot(outer.T, scaled, preferred_element_type=jnp.float32)
        outer_grad = jnp.dot(scaled, out_weight.T, preferred_element_type=jnp.float32).astype(jnp.bfloat16)
        outer_grad = outer_grad.reshape(block, R, C, C).astype(jnp.float32)
        left_part = jnp.einsum('ijcd,sjd->sic', outer_grad, right_full)
        right_grad = right_grad + jnp.einsum('ijcd,sic->sjd', outer_grad, left_block)
        return ((weight_grad, right_grad), (pair.reshape(block, R, PAIR), left_part))
    starts = jnp.arange(0, R, block, dtype=jnp.int32)
    start_carry = (jnp.zeros((C * C, PAIR), jnp.float32), jnp.zeros((SEQS, R, C), jnp.float32))
    (weight_grad, right_grad), (pairs, left_parts) = lax.scan(step, start_carry, starts)
    pair_update = pairs.reshape(R, R // RES_DEV, RES_DEV, PAIR)
    left_grad = jnp.transpose(left_parts, (1, 0, 2, 3)).reshape(SEQS, R, C)
    alignment_grad = norm_backward(normal_rows, inverse, weights, left_grad, right_grad, left_weight, right_weight)
    return (pair_update, alignment_grad, weight_grad)
```

```python
import jax
import jax.numpy as jnp
from jax import lax
from jax.experimental import pallas as pl
from jax.experimental.pallas import tpu as pltpu
from jax.sharding import PartitionSpec as P

F32 = jnp.float32
BF16 = jnp.bfloat16
MESH = pl.DeviceIdType.MESH

NX, NZ, NYZ = 4, 4, 16
NSEQ = NX * NZ
SEQS, RES, WIDTH, CH, PAIR = 32, 64, 32, 256, 128
COLS = 128
BLOCK = 8
NT_DIMS = (((1,), (1,)), ((), ()))


def iota(shape, dim):
    return lax.broadcasted_iota(jnp.int32, shape, dim)


def onehot(condition, kind=BF16):
    return jnp.where(condition, 1.0, 0.0).astype(kind)


def mm(a, b):
    return jnp.dot(a, b, preferred_element_type=F32)


def mm_nt(a, b):
    return lax.dot_general(a, b, NT_DIMS, preferred_element_type=F32)


def place():
    a = lax.axis_index("seq")
    b = lax.axis_index("res")
    x, zh = a // NZ, a % NZ
    core, yz = b % 2, b // 2
    return a, b, x, zh, core, yz


def partners_barrier(a, b, x, zh, core, yz):
    sem = pltpu.get_barrier_semaphore()

    def signal(seq, res):
        pl.semaphore_signal(sem, inc=1, device_id=(seq, res), device_id_type=MESH)

    for k in range(1, NZ):
        signal(x * NZ + (zh + k) % NZ, b)
    for k in range(1, NX):
        signal(((x + k) % NX) * NZ + zh, b)
    signal(a, yz * 2 + (1 - core))

    @pl.loop(1, NYZ)
    def _(k):
        signal(a, ((yz + k) % NYZ) * 2 + core)

    pl.semaphore_wait(sem, (NZ - 1) + (NX - 1) + 1 + (NYZ - 1))


def remote(src, dst, send, recv, seq, res):
    return pltpu.make_async_remote_copy(
        src_ref=src, dst_ref=dst, send_sem=send, recv_sem=recv, device_id=(seq, res), device_id_type=MESH
    )


def normalise(al_ref):
    values = al_ref[...].astype(F32)
    center = values - jnp.mean(values, -1, keepdims=True)
    inverse = lax.rsqrt(jnp.mean(center * center, -1, keepdims=True) + 1e-05)
    return center * inverse, inverse


def weight_rows(am_ref, rm_ref):
    return (am_ref[...] * rm_ref[...]).astype(F32)


def as_column(row):
    n = row.shape[1]
    return jnp.sum(jnp.where(iota((n, n), 0) == iota((n, n), 1), row, 0.0), axis=1, keepdims=True)


def gather_kernel(
    al_ref, am_ref, rm_ref, wl_ref, wr_ref, g_ref, x_ref, mask_ref,
    z_send, z_recv, x_send, x_recv, r_send, r_recv, c_send, c_recv,
):
    a, b, x, zh, core, yz = place()
    partners_barrier(a, b, x, zh, core, yz)
    normal, _ = normalise(al_ref)
    rounded = normal.astype(BF16)
    w2 = weight_rows(am_ref, rm_ref)
    total = jnp.zeros((RES, 128), F32)
    for s in range(2):
        lane, row = iota((WIDTH, 128), 1), iota((WIDTH, 128), 0)
        left_at = onehot(lane == row + s * WIDTH)
        right_at = onehot(lane == row + 2 * WIDTH + s * WIDTH)
        both = (mm(wl_ref[...], left_at) + mm(wr_ref[...], right_at)).astype(BF16)
        total = total + as_column(w2[s : s + 1]) * mm(rounded[s * RES : (s + 1) * RES], both)
    mask_ref[...] = jnp.zeros((16, 128), F32)
    mask_ref[0:2, 0:RES] = w2
    g_ref[a, 0:RES] = total.astype(BF16)
    g_ref[a, RES : RES + 16] = mask_ref[...].astype(BF16)

    def z_copy(k):
        other = (zh + k) % NZ
        return remote(g_ref.at[a], g_ref.at[a], z_send.at[k], z_recv.at[zh], x * NZ + other, b)

    for k in range(1, NZ):
        z_copy(k).start()
    for k in range(1, NZ):
        other = (zh + k) % NZ
        slot = g_ref.at[x * NZ + other]
        remote(slot, slot, z_send.at[k], z_recv.at[other], a, b).wait_recv()

    def x_copy(k):
        slab = g_ref.at[pl.ds(x * NZ, NZ)]
        return remote(slab, slab, x_send.at[k], x_recv.at[x], ((x + k) % NX) * NZ + zh, b)

    for k in range(1, NX):
        x_copy(k).start()
    for k in range(1, NX):
        other = (x + k) % NX
        slab = g_ref.at[pl.ds(other * NZ, NZ)]
        remote(slab, slab, x_send.at[k], x_recv.at[other], a, b).wait_recv()

    blocks = g_ref[:, 0:RES, :].reshape(NSEQ * RES, 128)
    r, col = iota((64, NSEQ * RES), 0), iota((64, NSEQ * RES), 1)
    target = (2 * ((r % 32) // 4) + r // 32) * RES + 4 * a + r % 4
    picked = mm(onehot(col == target), blocks)
    even = pltpu.roll(picked[0:32], 64, 1)
    chunk = jnp.where(iota((32, 128), 1) < 64, even, picked[32:64])
    masks = g_ref[:, RES : RES + 16, :].astype(F32)[:, 0:8, :].reshape(128, 128).astype(BF16)
    r, lane = iota((16, 128), 0), iota((16, 128), 1)
    chunk_mask = mm_nt(onehot((lane == 4 * a + r) & (r < 4)), masks)
    x_ref[core, yz, 0:32] = chunk.astype(BF16)
    x_ref[core, yz, 32:48] = chunk_mask.astype(BF16)

    def r_copy(k):
        other = (yz + k) % NYZ
        slot = x_ref.at[core, yz]
        return remote(slot, slot, r_send.at[k], r_recv.at[yz], a, other * 2 + core)

    @pl.loop(1, NYZ)
    def _(k):
        r_copy(k).start()

    @pl.loop(1, NYZ)
    def _(k):
        other = (yz + k) % NYZ
        slot = x_ref.at[core, other]
        remote(slot, slot, r_send.at[k], r_recv.at[other], a, b).wait_recv()

    c_copy = remote(x_ref.at[core], x_ref.at[core], c_send, c_recv, a, yz * 2 + (1 - core))
    c_copy.start()
    for k in range(1, NZ):
        z_copy(k).wait_send()
    for k in range(1, NX):
        x_copy(k).wait_send()

    @pl.loop(1, NYZ)
    def _(k):
        r_copy(k).wait_send()

    c_copy.wait_send()
    slab = x_ref.at[1 - core]
    remote(slab, slab, c_send, c_recv, a, b).wait_recv()


def pair_kernel(
    g_ref, x_ref, w_ref, ct_ref, pair_ref, lm_ref, rd_ref,
    wf, wn, w4, lf, l2, lt, rf, rmf, perm, rds, rt, rden, nc, tb, sc, rg, lgs, dw,
):
    step = pl.program_id(0)

    @pl.when(step == 0)
    def _():
        wf[...] = w_ref[...].astype(F32)
        for d in range(WIDTH):
            piece = wf[pl.ds(d, WIDTH, stride=WIDTH), :].astype(BF16)
            wn[:, d * PAIR : (d + 1) * PAIR] = piece
            for q in range(4):
                w4[q * WIDTH : (q + 1) * WIDTH, d * PAIR : (d + 1) * PAIR] = piece
        blocks = g_ref[:, 0:RES, :].reshape(NSEQ * RES, 128)
        row, lane = iota((128, 128), 0), iota((128, 128), 1)
        for s in range(2):
            moved = mm(blocks, onehot((row == lane + s * WIDTH) & (lane < WIDTH)))
            for n in range(NSEQ):
                lf[pl.ds(2 * n + s, RES, stride=SEQS), :] = moved[n * RES : (n + 1) * RES]
        l2[...] = lf[...].astype(BF16)
        eye = onehot(iota((WIDTH, 128), 0) == iota((WIDTH, 128), 1))
        for n in range(RES // BLOCK):
            rows = BLOCK * SEQS
            lt[n] = mm_nt(eye, l2[n * rows : (n + 1) * rows, :]).astype(BF16)
        for core in range(2):
            for yz in range(NYZ):
                part = x_ref[core, yz].astype(F32)
                at = (yz * 2 + core) * 4
                for t in range(8):
                    rf[at : at + 4, t * 128 : (t + 1) * 128] = part[4 * t : 4 * t + 4]
                rmf[at : at + 4, :] = part[32:36]
        size = WIDTH * SEQS
        for n in range(8):
            r, col = iota((size // 8, size), 0) + n * (size // 8), iota((size // 8, size), 1)
            perm[n * (size // 8) : (n + 1) * (size // 8), :] = onehot(col == (r % 32) * 32 + r // 32)
        right = rf[...].astype(BF16)
        rds[...] = mm(right, perm[...]).astype(BF16)
        rt[...] = mm_nt(perm[...], right).astype(BF16)
        masks = g_ref[:, RES : RES + 16, :].astype(F32)[:, 0:8, :].reshape(128, 128).astype(BF16)
        counts = mm(rmf[...].astype(BF16), masks)
        rden[...] = 1.0 / jnp.maximum(counts, 1.0)
        rg[...] = jnp.zeros_like(rg)
        dw[...] = jnp.zeros_like(dw)

    rows = BLOCK * SEQS
    l2c = l2[pl.ds(pl.multiple_of(step * rows, rows), rows), 0:WIDTH]
    scale = pltpu.roll(rden[...], lax.rem(128 - step * BLOCK, 128), 1)
    for d2 in range(WIDTH // 2):
        part = mm(l2c, wn[:, d2 * 256 : (d2 + 1) * 256]).astype(BF16)
        for h in range(2):
            d = 2 * d2 + h
            for k in range(BLOCK):
                nc[d * SEQS : (d + 1) * SEQS, k * PAIR : (k + 1) * PAIR] = part[
                    k * SEQS : (k + 1) * SEQS, h * PAIR : (h + 1) * PAIR
                ]
    for k in range(BLOCK):
        sc[:, k * PAIR : (k + 1) * PAIR] = (ct_ref[k].astype(F32) * scale[:, k : k + 1]).astype(BF16)
    for k2 in range(BLOCK // 2):
        part = mm(rds[...], nc[:, k2 * 256 : (k2 + 1) * 256])
        for h in range(2):
            k = 2 * k2 + h
            pair_ref[k] = (part[:, h * PAIR : (h + 1) * PAIR] * scale[:, k : k + 1]).astype(BF16)
    rg[...] += mm_nt(sc[...], nc[...])
    for k2 in range(BLOCK // 2):
        part = mm(rt[...], sc[:, k2 * 256 : (k2 + 1) * 256]).astype(BF16)
        for h in range(2):
            k = 2 * k2 + h
            for d in range(WIDTH):
                tb[k * SEQS : (k + 1) * SEQS, d * PAIR : (d + 1) * PAIR] = part[
                    d * SEQS : (d + 1) * SEQS, h * PAIR : (h + 1) * PAIR
                ]
    lgs[pl.ds(pl.multiple_of(step * rows, rows), rows), :] = mm_nt(tb[...], w4[...])
    dw[...] += mm(lt[step], tb[...])

    @pl.when(step == pl.num_programs(0) - 1)
    def _():
        rf[...] = mm(rg[...].astype(BF16), perm[...])
        for core in range(2):
            for yz in range(NYZ):
                d = yz * 2 + core
                lf[0:32, :] = jnp.concatenate(
                    [rf[4 * d : 4 * d + 4, t * 128 : (t + 1) * 128] for t in range(8)], axis=0
                )
                rd_ref[core, yz, 0:32] = lf[0:32, :].astype(BF16)
                rd_ref[core, yz, 32:64] = dw[:, d * PAIR : (d + 1) * PAIR].astype(BF16)
        lane = iota((32, 128), 1) // WIDTH
        for n in range(NSEQ):
            out = lgs[pl.ds(2 * n, 32, stride=SEQS), :]
            for q in range(1, 4):
                piece = lgs[pl.ds((q // 2) * 32 * SEQS + 2 * n + q % 2, 32, stride=SEQS), :]
                out = jnp.where(lane == q, piece, out)
            lm_ref[n] = out.astype(BF16)


def reduce_kernel(
    rd_ref, lm_ref, al_ref, am_ref, rm_ref, wl_ref, wr_ref, ag_ref, dw_ref,
    core_in, half, half_in, seq_all, left_x, left_half, left_z, fin,
    c_send, c_recv, lx_send, lx_recv, r_send, r_recv, lz_send, lz_recv,
    z_send, z_recv, x_send, x_recv, f_send, f_recv, e_send, e_recv,
):
    a, b, x, zh, core, yz = place()
    partners_barrier(a, b, x, zh, core, yz)
    c_copy = remote(rd_ref.at[1 - core], core_in, c_send, c_recv, a, yz * 2 + (1 - core))
    c_copy.start()

    def lx_copy(k):
        other = (x + k) % NX
        return remote(
            lm_ref.at[pl.ds(other * NZ, NZ)], left_x.at[x], lx_send.at[k], lx_recv.at[x], other * NZ + zh, b
        )

    for k in range(1, NX):
        lx_copy(k).start()
    c_copy.wait_recv()
    for n in range(NYZ):
        half[n] = (rd_ref[core, n].astype(F32) + core_in[n].astype(F32)).astype(BF16)

    def r_copy(k):
        other = (yz + k) % NYZ
        return remote(half.at[other], half_in.at[yz], r_send.at[k], r_recv.at[yz], a, other * 2 + core)

    @pl.loop(1, NYZ)
    def _(k):
        r_copy(k).start()

    half_in[yz] = half[yz]
    left_x[x] = lm_ref[pl.ds(x * NZ, NZ)]
    for k in range(1, NX):
        other = (x + k) % NX
        slab = left_x.at[other]
        remote(slab, slab, lx_send.at[k], lx_recv.at[other], a, b).wait_recv()
    left = left_x[0].astype(F32)
    for n in range(1, NX):
        left = left + left_x[n].astype(F32)
    left_half[...] = left.astype(BF16)

    def lz_copy(k):
        other = (zh + k) % NZ
        return remote(left_half.at[other], left_z.at[zh], lz_send.at[k], lz_recv.at[zh], x * NZ + other, b)

    for k in range(1, NZ):
        lz_copy(k).start()
    left_z[zh] = left_half[zh]

    @pl.loop(1, NYZ)
    def _(k):
        other = (yz + k) % NYZ
        slot = half_in.at[other]
        remote(slot, slot, r_send.at[k], r_recv.at[other], a, b).wait_recv()

    chunk = half_in[0].astype(F32)
    for n in range(1, NYZ):
        chunk = chunk + half_in[n].astype(F32)
    seq_all[a] = chunk.astype(BF16)

    def z_copy(k):
        other = (zh + k) % NZ
        return remote(seq_all.at[a], seq_all.at[a], z_send.at[k], z_recv.at[zh], x * NZ + other, b)

    for k in range(1, NZ):
        z_copy(k).start()
    for k in range(1, NZ):
        other = (zh + k) % NZ
        slot = seq_all.at[x * NZ + other]
        remote(slot, slot, z_send.at[k], z_recv.at[other], a, b).wait_recv()

    def x_copy(k):
        slab = seq_all.at[pl.ds(x * NZ, NZ)]
        return remote(slab, slab, x_send.at[k], x_recv.at[x], ((x + k) % NX) * NZ + zh, b)

    for k in range(1, NX):
        x_copy(k).start()
    for k in range(1, NZ):
        other = (zh + k) % NZ
        slot = left_z.at[other]
        remote(slot, slot, lz_send.at[k], lz_recv.at[other], a, b).wait_recv()
    left = left_z[0].astype(F32)
    for n in range(1, NZ):
        left = left + left_z[n].astype(F32)
    normal, inverse = normalise(al_ref)
    w2 = weight_rows(am_ref, rm_ref)
    for k in range(1, NX):
        other = (x + k) % NX
        slab = seq_all.at[pl.ds(other * NZ, NZ)]
        remote(slab, slab, x_send.at[k], x_recv.at[other], a, b).wait_recv()

    block = seq_all[0, 32:64].astype(F32)
    for n in range(1, NSEQ):
        block = block + seq_all[n, 32:64].astype(F32)
    fin[core, yz] = block.astype(BF16)

    def f_copy(k):
        other = (yz + k) % NYZ
        slot = fin.at[core, yz]
        return remote(slot, slot, f_send.at[k], f_recv.at[yz], a, other * 2 + core)

    @pl.loop(1, NYZ)
    def _(k):
        f_copy(k).start()

    rows = seq_all[:, 0:32, :].reshape(NSEQ * 32, 128)
    r, col = iota((RES, NSEQ * 32), 0), iota((RES, NSEQ * 32), 1)
    right = mm(onehot(col == (r // 4) * 32 + (a // 2) * 4 + r % 4), rows).astype(BF16)
    left_high = left.astype(BF16)
    left_low = (left - left_high.astype(F32)).astype(BF16)
    row, lane = iota((128, WIDTH), 0), iota((128, WIDTH), 1)
    for s in range(2):
        right_at = mm_nt(onehot(row == lane + (a % 2) * 64 + s * WIDTH), wr_ref[...]).astype(BF16)
        parts = []
        for h in range(2):
            left_at = mm_nt(onehot(row == lane + (2 * h + s) * WIDTH), wl_ref[...]).astype(BF16)
            parts.append(mm(left_high, left_at) + mm(left_low, left_at))
        grad = (jnp.concatenate(parts, axis=0) + mm(right, right_at)) * as_column(w2[s : s + 1])
        span = slice(s * RES, (s + 1) * RES)
        first = jnp.mean(grad, -1, keepdims=True)
        second = jnp.mean(grad * normal[span], -1, keepdims=True)
        ag_ref[span] = (inverse[span] * (grad - first - normal[span] * second)).astype(BF16)

    @pl.loop(1, NYZ)
    def _(k):
        other = (yz + k) % NYZ
        slot = fin.at[core, other]
        remote(slot, slot, f_send.at[k], f_recv.at[other], a, b).wait_recv()

    e_copy = remote(fin.at[core], fin.at[core], e_send, e_recv, a, yz * 2 + (1 - core))
    e_copy.start()
    c_copy.wait_send()
    for k in range(1, NX):
        lx_copy(k).wait_send()
        x_copy(k).wait_send()
    for k in range(1, NZ):
        lz_copy(k).wait_send()
        z_copy(k).wait_send()

    @pl.loop(1, NYZ)
    def _(k):
        r_copy(k).wait_send()
        f_copy(k).wait_send()

    e_copy.wait_send()
    slab = fin.at[1 - core]
    remote(slab, slab, e_send, e_recv, a, b).wait_recv()
    for c in range(2):
        for n in range(NYZ):
            dw_ref[pl.ds(n * 2 + c, WIDTH, stride=WIDTH), :] = fin[c, n].astype(F32)


def vmem():
    return pl.BlockSpec(memory_space=pltpu.VMEM)


def whole(shape):
    return pl.BlockSpec(shape, lambda i: (0,) * len(shape))


def dma(n):
    return pltpu.SemaphoreType.DMA((n,))


def shards(alignment, align_mask, residue_mask, left_weight, right_weight, out_weight, pair_cotangent):
    al = alignment.reshape(2 * RES, CH)
    rm = residue_mask.reshape(1, RES)
    one = pltpu.SemaphoreType.DMA
    gathered, rights = pl.pallas_call(
        gather_kernel,
        out_shape=(
            jax.ShapeDtypeStruct((NSEQ, RES + 16, 128), BF16),
            jax.ShapeDtypeStruct((2, NYZ, 48, 128), BF16),
        ),
        in_specs=[vmem()] * 5,
        out_specs=(vmem(), vmem()),
        scratch_shapes=[
            pltpu.VMEM((16, 128), F32),
            dma(NZ), dma(NZ), dma(NX), dma(NX), dma(NYZ), dma(NYZ), one, one,
        ],
        compiler_params=pltpu.CompilerParams(
            collective_id=0, has_side_effects=True, vmem_limit_bytes=24 * 1024 * 1024
        ),
        name="gather_rows",
    )(al, align_mask, rm, left_weight, right_weight)

    steps = RES // BLOCK
    size = WIDTH * SEQS
    tile = pl.BlockSpec((BLOCK, COLS, PAIR), lambda i: (i, 0, 0))
    pair, left_msg, rd = pl.pallas_call(
        pair_kernel,
        grid=(steps,),
        out_shape=(
            jax.ShapeDtypeStruct((RES, COLS, PAIR), BF16),
            jax.ShapeDtypeStruct((NSEQ, 32, 128), BF16),
            jax.ShapeDtypeStruct((2, NYZ, 64, 128), BF16),
        ),
        in_specs=[whole(gathered.shape), whole(rights.shape), whole((size, PAIR)), tile],
        out_specs=(tile, whole((NSEQ, 32, 128)), whole((2, NYZ, 64, 128))),
        scratch_shapes=[
            pltpu.VMEM((size, PAIR), F32),
            pltpu.VMEM((WIDTH, WIDTH * PAIR), BF16),
            pltpu.VMEM((128, WIDTH * PAIR), BF16),
            pltpu.VMEM((RES * SEQS, 128), F32),
            pltpu.VMEM((RES * SEQS, 128), BF16),
            pltpu.VMEM((steps, WIDTH, BLOCK * SEQS), BF16),
            pltpu.VMEM((COLS, size), F32),
            pltpu.VMEM((COLS, 128), F32),
            pltpu.VMEM((size, size), BF16),
            pltpu.VMEM((COLS, size), BF16),
            pltpu.VMEM((size, COLS), BF16),
            pltpu.VMEM((COLS, 128), F32),
            pltpu.VMEM((size, BLOCK * PAIR), BF16),
            pltpu.VMEM((BLOCK * SEQS, WIDTH * PAIR), BF16),
            pltpu.VMEM((COLS, BLOCK * PAIR), BF16),
            pltpu.VMEM((COLS, size), F32),
            pltpu.VMEM((RES * SEQS, 128), F32),
            pltpu.VMEM((WIDTH, WIDTH * PAIR), F32),
        ],
        compiler_params=pltpu.CompilerParams(vmem_limit_bytes=48 * 1024 * 1024),
        name="pair_update",
    )(gathered, rights, out_weight, pair_cotangent.reshape(RES, COLS, PAIR))

    ag, dw = pl.pallas_call(
        reduce_kernel,
        out_shape=(
            jax.ShapeDtypeStruct((2 * RES, CH), BF16),
            jax.ShapeDtypeStruct((size, PAIR), F32),
        ),
        in_specs=[vmem()] * 7,
        out_specs=(vmem(), vmem()),
        scratch_shapes=[
            pltpu.VMEM((NYZ, 64, 128), BF16),
            pltpu.VMEM((NYZ, 64, 128), BF16),
            pltpu.VMEM((NYZ, 64, 128), BF16),
            pltpu.VMEM((NSEQ, 64, 128), BF16),
            pltpu.VMEM((NX, NZ, 32, 128), BF16),
            pltpu.VMEM((NZ, 32, 128), BF16),
            pltpu.VMEM((NZ, 32, 128), BF16),
            pltpu.VMEM((2, NYZ, 32, 128), BF16),
            one, one, dma(NX), dma(NX), dma(NYZ), dma(NYZ), dma(NZ), dma(NZ),
            dma(NZ), dma(NZ), dma(NX), dma(NX), dma(NYZ), dma(NYZ), one, one,
        ],
        compiler_params=pltpu.CompilerParams(
            collective_id=1, has_side_effects=True, vmem_limit_bytes=24 * 1024 * 1024
        ),
        name="reduce_gradients",
    )(rd, left_msg, al, align_mask, rm, left_weight, right_weight)
    return (
        pair.reshape(pair_cotangent.shape),
        ag.reshape(alignment.shape),
        dw,
    )


def solution(mesh):
    in_specs = (
        P("seq", "res", None),
        P("seq", "res"),
        P("res"),
        P(),
        P(),
        P(),
        P("res", None, "seq", None),
    )
    out_specs = (P("res", None, "seq", None), P("seq", "res", None), P())
    return jax.shard_map(shards, mesh=mesh, in_specs=in_specs, out_specs=out_specs, check_vma=False)
```

```python
import jax
import jax.numpy as jnp
from jax import lax
from jax.experimental import pallas as pl
from jax.experimental.pallas import tpu as pltpu
from jax.sharding import PartitionSpec as P

F32 = jnp.float32
BF16 = jnp.bfloat16
MESH = pl.DeviceIdType.MESH

NSEQ, SEQS, RES, WIDTH, CH, PAIR, COLS = 16, 32, 64, 32, 256, 128, 128
BLOCK = 8
STEPS = RES // BLOCK
SIZE = WIDTH * SEQS
NT_DIMS = (((1,), (1,)), ((), ()))


def iota(shape, dim):
    return lax.broadcasted_iota(jnp.int32, shape, dim)


def onehot(condition):
    return jnp.where(condition, 1.0, 0.0).astype(BF16)


def mm(a, b):
    return jnp.dot(a, b, preferred_element_type=F32)


def mm_nt(a, b):
    return lax.dot_general(a, b, NT_DIMS, preferred_element_type=F32)


def split(value):
    high = value.astype(BF16)
    return high, (value - high.astype(F32)).astype(BF16)


def as_column(row):
    n = row.shape[1]
    return jnp.sum(jnp.where(iota((n, n), 0) == iota((n, n), 1), row, 0.0), axis=1, keepdims=True)


def remote(src, dst, send, recv, device):
    return pltpu.make_async_remote_copy(
        src_ref=src, dst_ref=dst, send_sem=send, recv_sem=recv, device_id=device, device_id_type=MESH
    )


class Group:
    def __init__(self, count, me, device_of, source_of, slot_of, send, recv):
        self.count, self.me, self.device_of = count, me, device_of
        self.source_of, self.slot_of, self.send, self.recv = source_of, slot_of, send, recv

    def each(self, body):
        if self.count <= 4:
            for k in range(1, self.count):
                body(k, (self.me + k) % self.count)
        else:

            @pl.loop(1, self.count)
            def _(k):
                body(k, (self.me + k) % self.count)

    def out(self, k, other):
        return remote(
            self.source_of(other), self.slot_of(self.me), self.send.at[k], self.recv.at[self.me],
            self.device_of(other),
        )

    def start(self):
        self.each(lambda k, other: self.out(k, other).start())

    def wait(self):
        def body(k, other):
            slot = self.slot_of(other)
            remote(slot, slot, self.send.at[k], self.recv.at[other], self.device_of(other)).wait_recv()

        self.each(body)

    def sent(self):
        self.each(lambda k, other: self.out(k, other).wait_send())


def total(ref, first, count, span=slice(None)):
    value = ref[first, span].astype(F32)
    for n in range(1, count):
        value = value + ref[first + n, span].astype(F32)
    return value


def kernel(
    al_hbm, am_hbm, rm_hbm, wl_hbm, wr_hbm, w_hbm, ct_hbm,
    pair_ref, ag_ref, dw_ref,
    al_ref, am_ref, rm_ref, wl_ref, wr_ref, w_ref, ct_ref, in_sem,
    mask_ref, rsend, ra, rb, xr, lall,
    wf, wn, w4, lf, l2, lt, perm, rp, rm_all, rds, rt, rden, n_all, t_all, sc, rg, lgs, dw,
    wmsg, wcin, whalf, wxin, wz, fin,
    rmsg, rcin, rhalf, rxin, rzs, rzin,
    lmsg, lx, lhalf, lz,
    c_send, c_recv,
    z_r_send, z_r_recv, z_l_send, z_l_recv, xy_r_send, xy_r_recv, x_l_send, x_l_recv,
    xy_w_send, xy_w_recv, z_w_send, z_w_recv, xy_f_send, xy_f_recv,
    xy_g_send, xy_g_recv, z_g_send, z_g_recv, x_g_send, x_g_recv, zl_g_send, zl_g_recv,
):
    a = lax.axis_index("seq")
    b = lax.axis_index("res")
    x, zh, core, y, zl = a // 4, a % 4, b % 2, b // 8, (b // 2) % 4
    xy, z = x * 4 + y, zh * 4 + zl
    z_device = lambda o: (x * 4 + o // 4, (y * 4 + o % 4) * 2 + core)
    xy_device = lambda o: ((o // 4) * 4 + zh, ((o % 4) * 4 + zl) * 2 + core)
    zh_device = lambda o: (x * 4 + o, b)
    x_device = lambda o: (o * 4 + zh, b)
    other_core = (a, b + 1 - 2 * core)

    def core_copy(n, src, dst):
        return remote(src, dst, c_send.at[n], c_recv.at[n], other_core)

    loads = [
        pltpu.make_async_copy(src, dst, in_sem.at[n])
        for n, (src, dst) in enumerate(
            (
                (al_hbm, al_ref), (am_hbm, am_ref), (rm_hbm, rm_ref), (wl_hbm, wl_ref), (wr_hbm, wr_ref),
                (w_hbm, w_ref), (ct_hbm, ct_ref),
            )
        )
    ]
    for load in loads:
        load.start()
    barrier = pltpu.get_barrier_semaphore()

    @pl.loop(1, 16)
    def _(k):
        pl.semaphore_signal(barrier, inc=1, device_id=z_device((z + k) % 16), device_id_type=MESH)
        pl.semaphore_signal(barrier, inc=1, device_id=xy_device((xy + k) % 16), device_id_type=MESH)

    pl.semaphore_signal(barrier, inc=1, device_id=other_core, device_id_type=MESH)
    for load in loads[:5]:
        load.wait()

    values = al_ref[...].astype(F32)
    center = values - jnp.mean(values, -1, keepdims=True)
    inverse = lax.rsqrt(jnp.mean(center * center, -1, keepdims=True) + 1e-05)
    rounded = (center * inverse).astype(BF16)
    w2 = (am_ref[...] * rm_ref[...]).astype(F32)
    row, lane = iota((128, WIDTH), 0), iota((128, WIDTH), 1)
    lanes = iota((RES, 128), 1)
    right = jnp.zeros((RES, 128), F32)
    left = jnp.zeros((32, 128), F32)
    for s in range(2):
        column = as_column(w2[s : s + 1])
        mine = rounded[s * RES : (s + 1) * RES]
        right_at = mm(onehot(row == lane + s * WIDTH), wr_ref[...]).astype(BF16)
        right = right + column * (mm_nt(mine, right_at) + jnp.where(lanes == 2 * WIDTH + s, 1.0, 0.0))
        for h in range(2):
            left_at = mm(onehot(row == lane + (2 * h + s) * WIDTH), wl_ref[...]).astype(BF16)
            span = slice(h * 32, (h + 1) * 32)
            left = left + column[span] * mm_nt(mine[span], left_at)
    r, col = iota((RES, RES), 0), iota((RES, RES), 1)
    order = onehot(col == ((r // 4) % 4) * 16 + (r // 16) * 4 + r % 4)
    right = mm(order, right.astype(BF16)).astype(BF16)
    for n in range(4):
        rsend[n] = right[n * 16 : (n + 1) * 16]
    mask_ref[...] = jnp.zeros((16, 128), F32)
    mask_ref[0:2, 0:RES] = w2
    lall[a, 0:32] = left.astype(BF16)
    lall[a, 32:48] = mask_ref[...].astype(BF16)

    loads[5].wait()
    wf[...] = w_ref[...].astype(F32)
    for d in range(WIDTH):
        piece = wf[pl.ds(d, WIDTH, stride=WIDTH), :].astype(BF16)
        wn[:, d * PAIR : (d + 1) * PAIR] = piece
        for q in range(4):
            w4[q * WIDTH : (q + 1) * WIDTH, d * PAIR : (d + 1) * PAIR] = piece

    pl.semaphore_wait(barrier, 31)

    z_r = Group(16, z, z_device, lambda o: rsend.at[o // 4], lambda n: ra.at[n], z_r_send, z_r_recv)
    z_l = Group(
        4, zh, zh_device, lambda o: lall.at[a], lambda n: lall.at[x * 4 + n], z_l_send, z_l_recv
    )
    z_r.start()
    z_l.start()
    ra[z] = rsend[zh]
    for n in range(8):
        r, col = iota((SIZE // 8, SIZE), 0) + n * (SIZE // 8), iota((SIZE // 8, SIZE), 1)
        perm[n * (SIZE // 8) : (n + 1) * (SIZE // 8), :] = onehot(col == (r % 32) * 32 + r // 32)
    z_r.wait()

    r, col = iota((256, 256), 0), iota((256, 256), 1)
    order = onehot(col == ((r // 16) % 4) * 64 + ((r // 4) % 4) * 16 + (r // 64) * 4 + r % 4)
    moved = mm(order, ra[...].reshape(256, 128))
    lanes = iota((16, 128), 1)
    for n in range(4):
        part = [moved[n * 64 + h * 16 : n * 64 + (h + 1) * 16] for h in range(4)]
        masks = jnp.zeros((16, 128), F32)
        for h in range(4):
            own = jnp.where((lanes >= 64) & (lanes < 66), part[h], 0.0)
            masks = masks + pltpu.roll(own, (x * 8 + h * 2 + 64) % 128, 1)
        for t in range(2):
            tile = jnp.where(lanes < 64, part[2 * t], pltpu.roll(part[2 * t + 1], 64, 1))
            rb[n, t * 16 : (t + 1) * 16] = tile.astype(BF16)
        rb[n, 32:48] = masks.astype(BF16)
    xy_r = Group(16, xy, xy_device, lambda o: rb.at[o // 4], lambda n: xr.at[core, n], xy_r_send, xy_r_recv)
    x_l = Group(
        4, x, x_device, lambda o: lall.at[pl.ds(x * 4, 4)], lambda n: lall.at[pl.ds(n * 4, 4)],
        x_l_send, x_l_recv,
    )
    xy_r.start()
    xr[core, xy] = rb[x]
    z_l.wait()
    x_l.start()
    loads[6].wait()
    xy_r.wait()

    c_r = core_copy(0, xr.at[core], xr.at[core])
    c_r.start()
    x_l.wait()
    blocks = lall[:, 0:32, :].reshape(NSEQ * 32, 128)
    row, lane = iota((128, 128), 0), iota((128, 128), 1)
    for h in range(2):
        for s in range(2):
            moved = mm(blocks, onehot((row == lane + (2 * h + s) * WIDTH) & (lane < WIDTH)))
            for n in range(NSEQ):
                lf[pl.ds(h * 32 * SEQS + 2 * n + s, 32, stride=SEQS), :] = moved[n * 32 : (n + 1) * 32]
    l2[...] = lf[...].astype(BF16)
    eye = onehot(iota((WIDTH, 128), 0) == iota((WIDTH, 128), 1))
    rows = BLOCK * SEQS
    for n in range(STEPS):
        lt[n] = mm_nt(eye, l2[n * rows : (n + 1) * rows, :]).astype(BF16)
    masks = lall[:, 32:48, :].astype(F32)[:, 0:8, :].reshape(128, 128).astype(BF16)
    r, col = iota((128, 128), 0), iota((128, 128), 1)
    left_mask = mm(onehot((r < SEQS) & (col == (r // 2) * 8 + r % 2)), masks).astype(BF16)
    slab = xr.at[1 - core]
    core_copy(0, slab, slab).wait_recv()

    for c in range(2):
        for n in range(4):
            at = slice((c * 4 + n) * 16, (c * 4 + n + 1) * 16)
            rm_all[at] = sum(xr[c, m * 4 + n, 32:48].astype(F32) for m in range(4))
            for m in range(4):
                for t in range(2):
                    rp[at, m * 256 + t * 128 : m * 256 + (t + 1) * 128] = xr[
                        c, m * 4 + n, t * 16 : (t + 1) * 16
                    ]
    r, col = iota((128, 128), 0), iota((128, 128), 1)
    order = onehot(col == ((r // 4) % 2) * 64 + (r // 32) * 16 + ((r // 8) % 4) * 4 + r % 4)
    right_mask = mm(order, rm_all[...].astype(BF16)).astype(BF16)
    rden[...] = 1.0 / jnp.maximum(mm(right_mask, left_mask), 1.0)
    right = mm(order, rp[...]).astype(BF16)
    rds[...] = mm(right, perm[...]).astype(BF16)
    rt[...] = mm_nt(perm[...], right).astype(BF16)

    def scale_of(step):
        return pltpu.roll(rden[...], lax.rem(128 - step * BLOCK, 128), 1)

    dw[...] = jnp.zeros_like(dw)

    @pl.loop(0, STEPS)
    def _(step):
        scale = scale_of(step)
        for k in range(BLOCK):
            sc[step, :, k * PAIR : (k + 1) * PAIR] = (
                ct_ref[step * BLOCK + k].astype(F32) * scale[:, k : k + 1]
            ).astype(BF16)
        for k2 in range(BLOCK // 2):
            part = mm(rt[...], sc[step, :, k2 * 256 : (k2 + 1) * 256]).astype(BF16)
            for h in range(2):
                k = 2 * k2 + h
                for d in range(WIDTH):
                    t_all[step, k * SEQS : (k + 1) * SEQS, d * PAIR : (d + 1) * PAIR] = part[
                        d * SEQS : (d + 1) * SEQS, h * PAIR : (h + 1) * PAIR
                    ]
        dw[...] += mm(lt[step], t_all[step])

    for c in range(2):
        for n in range(16):
            d = c * 16 + n
            wmsg[c, n] = dw[:, d * PAIR : (d + 1) * PAIR].astype(BF16)
    c_w = core_copy(1, wmsg.at[1 - core], wcin)
    c_w.start()

    rg[...] = jnp.zeros_like(rg)

    def right_part(step):
        rows = BLOCK * SEQS
        l2c = l2[pl.ds(pl.multiple_of(step * rows, rows), rows), 0:WIDTH]
        for d2 in range(WIDTH // 2):
            part = mm(l2c, wn[:, d2 * 256 : (d2 + 1) * 256]).astype(BF16)
            for h in range(2):
                d = 2 * d2 + h
                for k in range(BLOCK):
                    n_all[step, d * SEQS : (d + 1) * SEQS, k * PAIR : (k + 1) * PAIR] = part[
                        k * SEQS : (k + 1) * SEQS, h * PAIR : (h + 1) * PAIR
                    ]
        rg[...] += mm_nt(sc[step], n_all[step])

    pl.loop(0, 3)(right_part)

    core_copy(1, wcin, wcin).wait_recv()
    for n in range(16):
        whalf[n] = (wmsg[core, n].astype(F32) + wcin[n].astype(F32)).astype(BF16)
    xy_w = Group(16, xy, xy_device, lambda o: whalf.at[o], lambda n: wxin.at[n], xy_w_send, xy_w_recv)
    xy_w.start()
    wxin[xy] = whalf[xy]

    pl.loop(3, STEPS)(right_part)
    grads = mm(rg[...].astype(BF16), perm[...]).astype(BF16)
    r, col = iota((128, 128), 0), iota((128, 128), 1)
    order = onehot(col == ((r // 16) % 4) * 32 + ((r // 4) % 4) * 8 + (r // 64) * 4 + r % 4)
    grads = mm(order, grads).astype(BF16)
    for c in range(2):
        for m in range(4):
            for n in range(4):
                at = slice((c * 4 + n) * 16, (c * 4 + n + 1) * 16)
                for t in range(2):
                    rmsg[c, m * 4 + n, t * 16 : (t + 1) * 16] = grads[
                        at, m * 256 + t * 128 : m * 256 + (t + 1) * 128
                    ]
    c_g = core_copy(2, rmsg.at[1 - core], rcin)
    c_g.start()

    xy_w.wait()
    wz[z] = total(wxin, 0, 16).astype(BF16)
    z_w = Group(16, z, z_device, lambda o: wz.at[z], lambda n: wz.at[n], z_w_send, z_w_recv)
    z_w.start()

    def left_part(step):
        rows = BLOCK * SEQS
        lgs[pl.ds(pl.multiple_of(step * rows, rows), rows), :] = mm_nt(t_all[step], w4[...])

    pl.loop(0, 4)(left_part)
    core_copy(2, rcin, rcin).wait_recv()
    for n in range(16):
        rhalf[n] = (rmsg[core, n].astype(F32) + rcin[n].astype(F32)).astype(BF16)
    xy_g = Group(16, xy, xy_device, lambda o: rhalf.at[o], lambda n: rxin.at[n], xy_g_send, xy_g_recv)
    xy_g.start()
    rxin[xy] = rhalf[xy]
    pl.loop(4, STEPS)(left_part)
    lane = iota((32, 128), 1) // WIDTH
    for n in range(NSEQ):
        out = lgs[pl.ds(2 * n, 32, stride=SEQS), :]
        for q in range(1, 4):
            piece = lgs[pl.ds((q // 2) * 32 * SEQS + 2 * n + q % 2, 32, stride=SEQS), :]
            out = jnp.where(lane == q, piece, out)
        lmsg[n] = out.astype(BF16)
    x_g = Group(
        4, x, x_device, lambda o: lmsg.at[pl.ds(o * 4, 4)], lambda n: lx.at[n], x_g_send, x_g_recv
    )
    x_g.start()
    lx[x] = lmsg[pl.ds(x * 4, 4)]

    def pair_part(step):
        scale = scale_of(step)
        for k2 in range(BLOCK // 2):
            part = mm(rds[...], n_all[step, :, k2 * 256 : (k2 + 1) * 256])
            for h in range(2):
                k = 2 * k2 + h
                pair_ref[step * BLOCK + k] = (
                    part[:, h * PAIR : (h + 1) * PAIR] * scale[:, k : k + 1]
                ).astype(BF16)

    pl.loop(0, 4)(pair_part)

    xy_g.wait()
    sums = [total(rxin, m * 4, 4).astype(BF16) for m in range(4)]
    r, col = iota((64, 64), 0), iota((64, 64), 1)
    order = onehot(col == ((r // 4) % 4) * 16 + (r // 16) * 4 + r % 4)
    for t in range(2):
        moved = mm(order, jnp.concatenate([v[t * 16 : (t + 1) * 16] for v in sums], axis=0))
        for h in range(2):
            own = moved if h == 0 else pltpu.roll(moved, 64, 1)
            for n in range(4):
                rzs[(2 * t + h) * 4 + n] = own[n * 16 : (n + 1) * 16].astype(BF16)
    z_g = Group(16, z, z_device, lambda o: rzs.at[o], lambda n: rzin.at[n], z_g_send, z_g_recv)
    z_g.start()
    rzin[z] = rzs[z]

    x_g.wait()
    lhalf[...] = total(lx, 0, 4).astype(BF16)
    zl_g = Group(4, zh, zh_device, lambda o: lhalf.at[o], lambda n: lz.at[n], zl_g_send, zl_g_recv)
    zl_g.start()
    lz[zh] = lhalf[zh]

    z_w.wait()
    fin[core, xy] = total(wz, 0, 16).astype(BF16)
    xy_f = Group(
        16, xy, xy_device, lambda o: fin.at[core, xy], lambda n: fin.at[core, n], xy_f_send, xy_f_recv
    )
    xy_f.start()
    pl.loop(4, STEPS)(pair_part)

    values = al_ref[...].astype(F32)
    center = values - jnp.mean(values, -1, keepdims=True)
    inverse = lax.rsqrt(jnp.mean(center * center, -1, keepdims=True) + 1e-05)
    normal = center * inverse
    w2 = (am_ref[...] * rm_ref[...]).astype(F32)
    zl_g.wait()
    left = split(total(lz, 0, 4))
    z_g.wait()
    r, col = iota((RES, RES), 0), iota((RES, RES), 1)
    order = onehot(col == ((r // 4) % 4) * 16 + (r // 16) * 4 + r % 4)
    right = split(jnp.concatenate([total(rzin, n * 4, 4) for n in range(4)], axis=0))
    right = [mm(order, v).astype(BF16) for v in right]
    row, lane = iota((128, WIDTH), 0), iota((128, WIDTH), 1)
    for s in range(2):
        right_at = mm(onehot(row == lane + s * WIDTH), wr_ref[...]).astype(BF16)
        parts = []
        for h in range(2):
            left_at = mm(onehot(row == lane + (2 * h + s) * WIDTH), wl_ref[...]).astype(BF16)
            parts.append(mm(left[0], left_at) + mm(left[1], left_at))
        grad = jnp.concatenate(parts, axis=0) + mm(right[0], right_at) + mm(right[1], right_at)
        grad = grad * as_column(w2[s : s + 1])
        span = slice(s * RES, (s + 1) * RES)
        first = jnp.mean(grad, -1, keepdims=True)
        second = jnp.mean(grad * normal[span], -1, keepdims=True)
        ag_ref[span] = (inverse[span] * (grad - first - normal[span] * second)).astype(BF16)

    xy_f.wait()
    c_f = core_copy(3, fin.at[core], fin.at[core])
    c_f.start()
    for group in (z_r, z_l, xy_r, x_l, xy_w, z_w, xy_f, xy_g, z_g, x_g, zl_g):
        group.sent()
    for copy in (c_r, c_w, c_g, c_f):
        copy.wait_send()
    slab = fin.at[1 - core]
    core_copy(3, slab, slab).wait_recv()
    for c in range(2):
        for n in range(16):
            dw_ref[pl.ds(c * 16 + n, WIDTH, stride=WIDTH), :] = fin[c, n].astype(F32)


def shards(alignment, align_mask, residue_mask, left_weight, right_weight, out_weight, pair_cotangent):
    dma = pltpu.SemaphoreType.DMA
    vmem = pltpu.VMEM
    pair, ag, dw = pl.pallas_call(
        kernel,
        out_shape=(
            jax.ShapeDtypeStruct((RES, COLS, PAIR), BF16),
            jax.ShapeDtypeStruct((2 * RES, CH), BF16),
            jax.ShapeDtypeStruct((SIZE, PAIR), F32),
        ),
        in_specs=[pl.BlockSpec(memory_space=pl.ANY)] * 7,
        out_specs=(pl.BlockSpec(memory_space=pltpu.VMEM),) * 3,
        scratch_shapes=[
            vmem((2 * RES, CH), BF16), vmem((2, RES), jnp.int32), vmem((1, RES), jnp.int32),
            vmem((WIDTH, CH), BF16), vmem((WIDTH, CH), BF16), vmem((SIZE, PAIR), BF16),
            vmem((RES, COLS, PAIR), BF16), dma((7,)),
            vmem((16, 128), F32), vmem((4, 16, 128), BF16), vmem((16, 16, 128), BF16),
            vmem((4, 48, 128), BF16), vmem((2, 16, 48, 128), BF16), vmem((NSEQ, 48, 128), BF16),
            vmem((SIZE, PAIR), F32), vmem((WIDTH, WIDTH * PAIR), BF16), vmem((128, WIDTH * PAIR), BF16),
            vmem((RES * SEQS, 128), F32), vmem((RES * SEQS, 128), BF16),
            vmem((STEPS, WIDTH, BLOCK * SEQS), BF16), vmem((SIZE, SIZE), BF16),
            vmem((COLS, SIZE), BF16), vmem((COLS, 128), F32), vmem((COLS, SIZE), BF16),
            vmem((SIZE, COLS), BF16), vmem((COLS, 128), F32),
            vmem((STEPS, SIZE, BLOCK * PAIR), BF16), vmem((STEPS, BLOCK * SEQS, WIDTH * PAIR), BF16),
            vmem((STEPS, COLS, BLOCK * PAIR), BF16), vmem((COLS, SIZE), F32),
            vmem((RES * SEQS, 128), F32), vmem((WIDTH, WIDTH * PAIR), F32),
            vmem((2, 16, 32, 128), BF16), vmem((16, 32, 128), BF16), vmem((16, 32, 128), BF16),
            vmem((16, 32, 128), BF16), vmem((16, 32, 128), BF16), vmem((2, 16, 32, 128), BF16),
            vmem((2, 16, 32, 128), BF16), vmem((16, 32, 128), BF16), vmem((16, 32, 128), BF16),
            vmem((16, 32, 128), BF16), vmem((16, 16, 128), BF16), vmem((16, 16, 128), BF16),
            vmem((NSEQ, 32, 128), BF16), vmem((4, 4, 32, 128), BF16), vmem((4, 32, 128), BF16),
            vmem((4, 32, 128), BF16),
            dma((4,)), dma((4,)),
            dma((16,)), dma((16,)), dma((4,)), dma((4,)), dma((16,)), dma((16,)), dma((4,)), dma((4,)),
            dma((16,)), dma((16,)), dma((16,)), dma((16,)), dma((16,)), dma((16,)),
            dma((16,)), dma((16,)), dma((16,)), dma((16,)), dma((4,)), dma((4,)), dma((4,)), dma((4,)),
        ],
        compiler_params=pltpu.CompilerParams(
            collective_id=0, has_side_effects=True, vmem_limit_bytes=58 * 1024 * 1024
        ),
        name="pair_update",
    )(
        alignment.reshape(2 * RES, CH), align_mask, residue_mask.reshape(1, RES), left_weight.T, right_weight.T,
        out_weight, pair_cotangent.reshape(RES, COLS, PAIR),
    )
    return pair.reshape(pair_cotangent.shape), ag.reshape(alignment.shape), dw


def solution(mesh):
    in_specs = (
        P("seq", "res", None),
        P("seq", "res"),
        P("res"),
        P(),
        P(),
        P(),
        P("res", None, "seq", None),
    )
    out_specs = (P("res", None, "seq", None), P("seq", "res", None), P())
    return jax.shard_map(shards, mesh=mesh, in_specs=in_specs, out_specs=out_specs, check_vma=False)
```

```python
import jax
import jax.numpy as jnp
from jax import lax
from jax.experimental import pallas as pl
from jax.experimental.pallas import tpu as pltpu
from jax.sharding import PartitionSpec as P

F32 = jnp.float32
BF16 = jnp.bfloat16
MESH = pl.DeviceIdType.MESH

NSEQ, SEQS, RES, WIDTH, CH, PAIR, COLS = 16, 32, 64, 32, 256, 128, 128
BLOCK = 8
STEPS = RES // BLOCK
SIZE = WIDTH * SEQS
NT_DIMS = (((1,), (1,)), ((), ()))


def iota(shape, dim):
    return lax.broadcasted_iota(jnp.int32, shape, dim)


def onehot(condition):
    return jnp.where(condition, 1.0, 0.0).astype(BF16)


def mm(a, b):
    return jnp.dot(a, b, preferred_element_type=F32)


def mm_nt(a, b):
    return lax.dot_general(a, b, NT_DIMS, preferred_element_type=F32)


def split(value):
    high = value.astype(BF16)
    return high, (value - high.astype(F32)).astype(BF16)


def as_column(row):
    n = row.shape[1]
    return jnp.sum(jnp.where(iota((n, n), 0) == iota((n, n), 1), row, 0.0), axis=1, keepdims=True)


def remote(src, dst, send, recv, device):
    return pltpu.make_async_remote_copy(
        src_ref=src, dst_ref=dst, send_sem=send, recv_sem=recv, device_id=device, device_id_type=MESH
    )


class Group:
    def __init__(self, count, me, device_of, source_of, slot_of, send, recv, peer_of=None):
        self.count, self.me, self.device_of = count, me, device_of
        self.peer_of = peer_of or (lambda k: (me + k) % count)
        self.source_of, self.slot_of, self.send, self.recv = source_of, slot_of, send, recv

    def each(self, body):
        if self.count <= 4:
            for k in (2, 1, 3) if self.count == 4 else (1,):
                body(k, self.peer_of(k))
        else:

            @pl.loop(0, self.count - 1)
            def _(k):
                body(k, self.peer_of(k))

    def out(self, k, other):
        return remote(
            self.source_of(other), self.slot_of(self.me), self.send.at[k], self.recv.at[self.me],
            self.device_of(other),
        )

    def start(self):
        self.each(lambda k, other: self.out(k, other).start())

    def wait(self):
        def body(k, other):
            slot = self.slot_of(other)
            remote(slot, slot, self.send.at[k], self.recv.at[other], self.device_of(other)).wait_recv()

        self.each(body)

    def sent(self):
        self.each(lambda k, other: self.out(k, other).wait_send())


def total(ref, first, count, span=slice(None)):
    value = ref[first, span].astype(F32)
    for n in range(1, count):
        value = value + ref[first + n, span].astype(F32)
    return value


def kernel(
    al_hbm, am_hbm, rm_hbm, wl_hbm, wr_hbm, w_hbm, ct_hbm,
    pair_ref, ag_ref, fin,
    al_ref, am_ref, rm_ref, wl_ref, wr_ref, w_ref, ct_ref, in_sem,
    mask_ref, rsend, ra, rb, xr, lall,
    wf, wn, w4, lf, l2, lt, perm, rp, rm_all, rds, rt, rden, n_all, t_all, sc, rg, lgs, dw,
    wmsg, wcin, whalf, wxin, wz,
    rmsg, rcin, rhalf, rxin, rzs, rzin,
    lmsg, lx, lhalf, lz,
    c_send, c_recv,
    z_r_send, z_r_recv, z_l_send, z_l_recv, xy_r_send, xy_r_recv, x_l_send, x_l_recv,
    xy_w_send, xy_w_recv, z_w_send, z_w_recv, xy_f_send, xy_f_recv,
    xy_g_send, xy_g_recv, z_g_send, z_g_recv, x_g_send, x_g_recv, zl_g_send, zl_g_recv,
):
    a = lax.axis_index("seq")
    b = lax.axis_index("res")
    x, zh, core, y, zl = a // 4, a % 4, b % 2, b // 8, (b // 2) % 4
    xy, z = x * 4 + y, zh * 4 + zl
    z_device = lambda o: (x * 4 + o // 4, (y * 4 + o % 4) * 2 + core)
    xy_device = lambda o: ((o // 4) * 4 + zh, ((o % 4) * 4 + zl) * 2 + core)
    zh_device = lambda o: (x * 4 + o, b)
    x_device = lambda o: (o * 4 + zh, b)
    core_device = lambda o: (a, (y * 4 + zl) * 2 + o)

    def z_peer(k):
        return (z + 8 + ((k + 1) // 2) * (2 * (k % 2) - 1) + 16) % 16

    def turn(m):
        return 2 + (m * (m + 1)) // 2

    def xy_peer(k):
        return ((x + turn(k // 4)) % 4) * 4 + (y + turn(k % 4)) % 4

    def z_group(source_of, slot_of, send, recv):
        return Group(16, z, z_device, source_of, slot_of, send, recv, z_peer)

    def xy_group(source_of, slot_of, send, recv):
        return Group(16, xy, xy_device, source_of, slot_of, send, recv, xy_peer)

    def core_group(n, source_of, slot_of):
        return Group(2, core, core_device, source_of, slot_of, c_send.at[n], c_recv.at[n])

    loads = [
        pltpu.make_async_copy(src, dst, in_sem.at[n])
        for n, (src, dst) in enumerate(
            (
                (al_hbm, al_ref), (am_hbm, am_ref), (rm_hbm, rm_ref), (wl_hbm, wl_ref), (wr_hbm, wr_ref),
                (w_hbm, w_ref), (ct_hbm, ct_ref),
            )
        )
    ]
    for load in loads:
        load.start()
    barrier = pltpu.get_barrier_semaphore()

    @pl.loop(0, 15)
    def _(k):
        pl.semaphore_signal(barrier, inc=1, device_id=z_device(z_peer(k)), device_id_type=MESH)
        pl.semaphore_signal(barrier, inc=1, device_id=xy_device(xy_peer(k)), device_id_type=MESH)

    pl.semaphore_signal(barrier, inc=1, device_id=core_device(1 - core), device_id_type=MESH)
    for load in loads[:5]:
        load.wait()
    values = al_ref[...].astype(F32)
    center = values - jnp.mean(values, -1, keepdims=True)
    inverse = lax.rsqrt(jnp.mean(center * center, -1, keepdims=True) + 1e-05)
    rounded = (center * inverse).astype(BF16)
    w2 = (am_ref[...] * rm_ref[...]).astype(F32)
    row, lane = iota((128, WIDTH), 0), iota((128, WIDTH), 1)
    lanes = iota((RES, 128), 1)
    right = jnp.zeros((RES, 128), F32)
    left = jnp.zeros((32, 128), F32)
    for s in range(2):
        column = as_column(w2[s : s + 1])
        mine = rounded[s * RES : (s + 1) * RES]
        right_at = mm(onehot(row == lane + s * WIDTH), wr_ref[...]).astype(BF16)
        right = right + column * (mm_nt(mine, right_at) + jnp.where(lanes == 2 * WIDTH + s, 1.0, 0.0))
        for h in range(2):
            left_at = mm(onehot(row == lane + (2 * h + s) * WIDTH), wl_ref[...]).astype(BF16)
            span = slice(h * 32, (h + 1) * 32)
            left = left + column[span] * mm_nt(mine[span], left_at)
    r, col = iota((RES, RES), 0), iota((RES, RES), 1)
    order = onehot(col == ((r // 4) % 4) * 16 + (r // 16) * 4 + r % 4)
    right = mm(order, right.astype(BF16)).astype(BF16)
    for n in range(4):
        rsend[n] = right[n * 16 : (n + 1) * 16]
    mask_ref[...] = jnp.zeros((16, 128), F32)
    mask_ref[0:2, 0:RES] = w2
    lall[a, 0:32] = left.astype(BF16)
    lall[a, 32:48] = mask_ref[...].astype(BF16)
    loads[5].wait()
    wf[...] = w_ref[...].astype(F32)
    for d in range(WIDTH):
        piece = wf[pl.ds(d, WIDTH, stride=WIDTH), :].astype(BF16)
        wn[:, d * PAIR : (d + 1) * PAIR] = piece
        for q in range(4):
            w4[q * WIDTH : (q + 1) * WIDTH, d * PAIR : (d + 1) * PAIR] = piece
    pl.semaphore_wait(barrier, 31)
    z_r = z_group(lambda o: rsend.at[o // 4], lambda n: ra.at[n], z_r_send, z_r_recv)
    z_l = Group(
        4, zh, zh_device, lambda o: lall.at[a], lambda n: lall.at[x * 4 + n], z_l_send, z_l_recv
    )
    z_r.start()
    z_l.start()
    ra[z] = rsend[zh]
    for n in range(8):
        r, col = iota((SIZE // 8, SIZE), 0) + n * (SIZE // 8), iota((SIZE // 8, SIZE), 1)
        perm[n * (SIZE // 8) : (n + 1) * (SIZE // 8), :] = onehot(col == (r % 32) * 32 + r // 32)
    z_r.wait()
    r, col = iota((256, 256), 0), iota((256, 256), 1)
    order = onehot(col == ((r // 16) % 4) * 64 + ((r // 4) % 4) * 16 + (r // 64) * 4 + r % 4)
    moved = mm(order, ra[...].reshape(256, 128))
    lanes = iota((16, 128), 1)
    for n in range(4):
        part = [moved[n * 64 + h * 16 : n * 64 + (h + 1) * 16] for h in range(4)]
        masks = jnp.zeros((16, 128), F32)
        for h in range(4):
            own = jnp.where((lanes >= 64) & (lanes < 66), part[h], 0.0)
            masks = masks + pltpu.roll(own, (x * 8 + h * 2 + 64) % 128, 1)
        for t in range(2):
            tile = jnp.where(lanes < 64, part[2 * t], pltpu.roll(part[2 * t + 1], 64, 1))
            rb[n, t * 16 : (t + 1) * 16] = tile.astype(BF16)
        rb[n, 32:48] = masks.astype(BF16)
    xy_r = xy_group(lambda o: rb.at[o // 4], lambda n: xr.at[core, n], xy_r_send, xy_r_recv)
    x_l = Group(
        4, x, x_device, lambda o: lall.at[pl.ds(x * 4, 4)], lambda n: lall.at[pl.ds(n * 4, 4)],
        x_l_send, x_l_recv,
    )
    xy_r.start()
    xr[core, xy] = rb[x]
    z_l.wait()
    x_l.start()
    loads[6].wait()
    xy_r.wait()
    c_r = core_group(0, lambda o: xr.at[core], lambda n: xr.at[n])
    c_r.start()
    x_l.wait()
    blocks = lall[:, 0:32, :].reshape(NSEQ * 32, 128)
    row, lane = iota((128, 128), 0), iota((128, 128), 1)
    for h in range(2):
        for s in range(2):
            moved = mm(blocks, onehot((row == lane + (2 * h + s) * WIDTH) & (lane < WIDTH)))
            for n in range(NSEQ):
                lf[pl.ds(h * 32 * SEQS + 2 * n + s, 32, stride=SEQS), :] = moved[n * 32 : (n + 1) * 32]
    l2[...] = lf[...].astype(BF16)
    eye = onehot(iota((WIDTH, 128), 0) == iota((WIDTH, 128), 1))
    rows = BLOCK * SEQS
    for n in range(STEPS):
        lt[n] = mm_nt(eye, l2[n * rows : (n + 1) * rows, :]).astype(BF16)
    masks = lall[:, 32:48, :].astype(F32)[:, 0:8, :].reshape(128, 128).astype(BF16)
    r, col = iota((128, 128), 0), iota((128, 128), 1)
    left_mask = mm(onehot((r < SEQS) & (col == (r // 2) * 8 + r % 2)), masks).astype(BF16)
    c_r.wait()
    for c in range(2):
        for n in range(4):
            at = slice((c * 4 + n) * 16, (c * 4 + n + 1) * 16)
            rm_all[at] = sum(xr[c, m * 4 + n, 32:48].astype(F32) for m in range(4))
            for m in range(4):
                for t in range(2):
                    rp[at, m * 256 + t * 128 : m * 256 + (t + 1) * 128] = xr[
                        c, m * 4 + n, t * 16 : (t + 1) * 16
                    ]
    r, col = iota((128, 128), 0), iota((128, 128), 1)
    order = onehot(col == ((r // 4) % 2) * 64 + (r // 32) * 16 + ((r // 8) % 4) * 4 + r % 4)
    right_mask = mm(order, rm_all[...].astype(BF16)).astype(BF16)
    rden[...] = 1.0 / jnp.maximum(mm(right_mask, left_mask), 1.0)
    right = mm(order, rp[...]).astype(BF16)
    rds[...] = mm(right, perm[...]).astype(BF16)
    rt[...] = mm_nt(perm[...], right).astype(BF16)

    def scale_of(step):
        return pltpu.roll(rden[...], lax.rem(128 - step * BLOCK, 128), 1)
    dw[...] = jnp.zeros_like(dw)

    @pl.loop(0, STEPS)
    def _(step):
        scale = scale_of(step)
        for k in range(BLOCK):
            sc[step, :, k * PAIR : (k + 1) * PAIR] = (
                ct_ref[step * BLOCK + k].astype(F32) * scale[:, k : k + 1]
            ).astype(BF16)
        for k2 in range(BLOCK // 2):
            part = mm(rt[...], sc[step, :, k2 * 256 : (k2 + 1) * 256]).astype(BF16)
            for h in range(2):
                k = 2 * k2 + h
                for d in range(WIDTH):
                    t_all[step, k * SEQS : (k + 1) * SEQS, d * PAIR : (d + 1) * PAIR] = part[
                        d * SEQS : (d + 1) * SEQS, h * PAIR : (h + 1) * PAIR
                    ]
        dw[...] += mm(lt[step], t_all[step])
    for c in range(2):
        for n in range(16):
            d = c * 16 + n
            wmsg[c, n] = dw[:, d * PAIR : (d + 1) * PAIR].astype(BF16)
    c_w = core_group(1, lambda o: wmsg.at[o], lambda n: wcin)
    c_w.start()
    rg[...] = jnp.zeros_like(rg)

    def right_part(step):
        rows = BLOCK * SEQS
        l2c = l2[pl.ds(pl.multiple_of(step * rows, rows), rows), 0:WIDTH]
        for d2 in range(WIDTH // 2):
            part = mm(l2c, wn[:, d2 * 256 : (d2 + 1) * 256]).astype(BF16)
            for h in range(2):
                d = 2 * d2 + h
                for k in range(BLOCK):
                    n_all[step, d * SEQS : (d + 1) * SEQS, k * PAIR : (k + 1) * PAIR] = part[
                        k * SEQS : (k + 1) * SEQS, h * PAIR : (h + 1) * PAIR
                    ]
        rg[...] += mm_nt(sc[step], n_all[step])

    pl.loop(0, 3)(right_part)
    c_w.wait()
    for n in range(16):
        whalf[n] = (wmsg[core, n].astype(F32) + wcin[n].astype(F32)).astype(BF16)
    xy_w = xy_group(lambda o: whalf.at[o], lambda n: wxin.at[n], xy_w_send, xy_w_recv)
    xy_w.start()
    wxin[xy] = whalf[xy]
    pl.loop(3, STEPS)(right_part)
    grads = mm(rg[...].astype(BF16), perm[...]).astype(BF16)
    r, col = iota((128, 128), 0), iota((128, 128), 1)
    order = onehot(col == ((r // 16) % 4) * 32 + ((r // 4) % 4) * 8 + (r // 64) * 4 + r % 4)
    grads = mm(order, grads).astype(BF16)
    for c in range(2):
        for m in range(4):
            for n in range(4):
                at = slice((c * 4 + n) * 16, (c * 4 + n + 1) * 16)
                for t in range(2):
                    rmsg[c, m * 4 + n, t * 16 : (t + 1) * 16] = grads[
                        at, m * 256 + t * 128 : m * 256 + (t + 1) * 128
                    ]
    c_g = core_group(2, lambda o: rmsg.at[o], lambda n: rcin)
    c_g.start()
    xy_w.wait()
    wz[z] = total(wxin, 0, 16).astype(BF16)
    z_w = z_group(lambda o: wz.at[z], lambda n: wz.at[n], z_w_send, z_w_recv)
    z_w.start()
    def left_part(step):
        rows = BLOCK * SEQS
        lgs[pl.ds(pl.multiple_of(step * rows, rows), rows), :] = mm_nt(t_all[step], w4[...])

    pl.loop(0, 4)(left_part)
    c_g.wait()
    for n in range(16):
        rhalf[n] = (rmsg[core, n].astype(F32) + rcin[n].astype(F32)).astype(BF16)
    xy_g = xy_group(lambda o: rhalf.at[o], lambda n: rxin.at[n], xy_g_send, xy_g_recv)
    xy_g.start()
    rxin[xy] = rhalf[xy]
    pl.loop(4, STEPS)(left_part)
    lane = iota((32, 128), 1) // WIDTH
    for n in range(NSEQ):
        out = lgs[pl.ds(2 * n, 32, stride=SEQS), :]
        for q in range(1, 4):
            piece = lgs[pl.ds((q // 2) * 32 * SEQS + 2 * n + q % 2, 32, stride=SEQS), :]
            out = jnp.where(lane == q, piece, out)
        lmsg[n] = out.astype(BF16)
    x_g = Group(
        4, x, x_device, lambda o: lmsg.at[pl.ds(o * 4, 4)], lambda n: lx.at[n], x_g_send, x_g_recv
    )
    x_g.start()
    lx[x] = lmsg[pl.ds(x * 4, 4)]
    def pair_part(step):
        scale = scale_of(step)
        for k2 in range(BLOCK // 2):
            part = mm(rds[...], n_all[step, :, k2 * 256 : (k2 + 1) * 256])
            for h in range(2):
                k = 2 * k2 + h
                pair_ref[step * BLOCK + k] = (
                    part[:, h * PAIR : (h + 1) * PAIR] * scale[:, k : k + 1]
                ).astype(BF16)

    pl.loop(0, 4)(pair_part)
    xy_g.wait()
    sums = [total(rxin, m * 4, 4).astype(BF16) for m in range(4)]
    r, col = iota((64, 64), 0), iota((64, 64), 1)
    order = onehot(col == ((r // 4) % 4) * 16 + (r // 16) * 4 + r % 4)
    for t in range(2):
        moved = mm(order, jnp.concatenate([v[t * 16 : (t + 1) * 16] for v in sums], axis=0))
        for h in range(2):
            own = moved if h == 0 else pltpu.roll(moved, 64, 1)
            for n in range(4):
                rzs[(2 * t + h) * 4 + n] = own[n * 16 : (n + 1) * 16].astype(BF16)
    z_g = z_group(lambda o: rzs.at[o], lambda n: rzin.at[n], z_g_send, z_g_recv)
    z_g.start()
    rzin[z] = rzs[z]
    x_g.wait()
    lhalf[...] = total(lx, 0, 4).astype(BF16)
    zl_g = Group(4, zh, zh_device, lambda o: lhalf.at[o], lambda n: lz.at[n], zl_g_send, zl_g_recv)
    zl_g.start()
    lz[zh] = lhalf[zh]
    z_w.wait()
    fin[core, xy] = total(wz, 0, 16).astype(BF16)
    xy_f = xy_group(lambda o: fin.at[core, xy], lambda n: fin.at[core, n], xy_f_send, xy_f_recv)
    xy_f.start()
    pl.loop(4, STEPS)(pair_part)
    values = al_ref[...].astype(F32)
    center = values - jnp.mean(values, -1, keepdims=True)
    inverse = lax.rsqrt(jnp.mean(center * center, -1, keepdims=True) + 1e-05)
    normal = center * inverse
    w2 = (am_ref[...] * rm_ref[...]).astype(F32)
    zl_g.wait()
    left = split(total(lz, 0, 4))
    z_g.wait()
    r, col = iota((RES, RES), 0), iota((RES, RES), 1)
    order = onehot(col == ((r // 4) % 4) * 16 + (r // 16) * 4 + r % 4)
    right = split(jnp.concatenate([total(rzin, n * 4, 4) for n in range(4)], axis=0))
    right = [mm(order, v).astype(BF16) for v in right]
    row, lane = iota((128, WIDTH), 0), iota((128, WIDTH), 1)
    for s in range(2):
        right_at = mm(onehot(row == lane + s * WIDTH), wr_ref[...]).astype(BF16)
        parts = []
        for h in range(2):
            left_at = mm(onehot(row == lane + (2 * h + s) * WIDTH), wl_ref[...]).astype(BF16)
            parts.append(mm(left[0], left_at) + mm(left[1], left_at))
        grad = jnp.concatenate(parts, axis=0) + mm(right[0], right_at) + mm(right[1], right_at)
        grad = grad * as_column(w2[s : s + 1])
        span = slice(s * RES, (s + 1) * RES)
        first = jnp.mean(grad, -1, keepdims=True)
        second = jnp.mean(grad * normal[span], -1, keepdims=True)
        ag_ref[span] = (inverse[span] * (grad - first - normal[span] * second)).astype(BF16)
    xy_f.wait()
    c_f = core_group(3, lambda o: fin.at[core], lambda n: fin.at[n])
    c_f.start()
    for group in (z_r, z_l, xy_r, x_l, c_r, c_w, c_g, xy_w, z_w, xy_f, xy_g, z_g, x_g, zl_g, c_f):
        group.sent()
    c_f.wait()


def write_kernel(pair_in, ag_in, fin_ref, pair_out, ag_out, dw_out, dw_ref, sem):
    parts = [
        pltpu.make_async_copy(pair_in.at[pl.ds(n * 8, 8)], pair_out.at[pl.ds(n * 8, 8)], sem.at[2 + n])
        for n in range(8)
    ]
    for part in parts:
        part.start()
    rows = pltpu.make_async_copy(ag_in, ag_out, sem.at[0])
    rows.start()
    for c in range(2):
        for n in range(16):
            dw_ref[pl.ds(c * 16 + n, WIDTH, stride=WIDTH), :] = fin_ref[c, n].astype(F32)
    grads = pltpu.make_async_copy(dw_ref, dw_out, sem.at[1])
    grads.start()
    for part in parts:
        part.wait()
    rows.wait()
    grads.wait()


def shards(alignment, align_mask, residue_mask, left_weight, right_weight, out_weight, pair_cotangent):
    dma = pltpu.SemaphoreType.DMA
    vmem = pltpu.VMEM
    pair, ag, fin = pl.pallas_call(
        kernel,
        out_shape=(
            jax.ShapeDtypeStruct((RES, COLS, PAIR), BF16),
            jax.ShapeDtypeStruct((2 * RES, CH), BF16),
            jax.ShapeDtypeStruct((2, 16, WIDTH, PAIR), BF16),
        ),
        in_specs=[pl.BlockSpec(memory_space=pltpu.HBM)] * 7,
        out_specs=(pl.BlockSpec(memory_space=pltpu.VMEM),) * 3,
        scratch_shapes=[
            vmem((2 * RES, CH), BF16), vmem((2, RES), jnp.int32), vmem((1, RES), jnp.int32),
            vmem((WIDTH, CH), BF16), vmem((WIDTH, CH), BF16), vmem((SIZE, PAIR), BF16),
            vmem((RES, COLS, PAIR), BF16), dma((7,)),
            vmem((16, 128), F32), vmem((4, 16, 128), BF16), vmem((16, 16, 128), BF16),
            vmem((4, 48, 128), BF16), vmem((2, 16, 48, 128), BF16), vmem((NSEQ, 48, 128), BF16),
            vmem((SIZE, PAIR), F32), vmem((WIDTH, WIDTH * PAIR), BF16), vmem((128, WIDTH * PAIR), BF16),
            vmem((RES * SEQS, 128), F32), vmem((RES * SEQS, 128), BF16),
            vmem((STEPS, WIDTH, BLOCK * SEQS), BF16), vmem((SIZE, SIZE), BF16),
            vmem((COLS, SIZE), BF16), vmem((COLS, 128), F32), vmem((COLS, SIZE), BF16),
            vmem((SIZE, COLS), BF16), vmem((COLS, 128), F32),
            vmem((STEPS, SIZE, BLOCK * PAIR), BF16), vmem((STEPS, BLOCK * SEQS, WIDTH * PAIR), BF16),
            vmem((STEPS, COLS, BLOCK * PAIR), BF16), vmem((COLS, SIZE), F32),
            vmem((RES * SEQS, 128), F32), vmem((WIDTH, WIDTH * PAIR), F32),
            vmem((2, 16, 32, 128), BF16), vmem((16, 32, 128), BF16), vmem((16, 32, 128), BF16),
            vmem((16, 32, 128), BF16), vmem((16, 32, 128), BF16),
            vmem((2, 16, 32, 128), BF16), vmem((16, 32, 128), BF16), vmem((16, 32, 128), BF16),
            vmem((16, 32, 128), BF16), vmem((16, 16, 128), BF16), vmem((16, 16, 128), BF16),
            vmem((NSEQ, 32, 128), BF16), vmem((4, 4, 32, 128), BF16), vmem((4, 32, 128), BF16),
            vmem((4, 32, 128), BF16),
            dma((4, 2)), dma((4, 2)),
            dma((16,)), dma((16,)), dma((4,)), dma((4,)), dma((16,)), dma((16,)), dma((4,)), dma((4,)),
            dma((16,)), dma((16,)), dma((16,)), dma((16,)), dma((16,)), dma((16,)),
            dma((16,)), dma((16,)), dma((16,)), dma((16,)), dma((4,)), dma((4,)), dma((4,)), dma((4,)),
        ],
        compiler_params=pltpu.CompilerParams(
            collective_id=0, has_side_effects=True, vmem_limit_bytes=60000000
        ),
        name="pair_update",
    )(
        alignment.reshape(2 * RES, CH), align_mask, residue_mask.reshape(1, RES), left_weight.T, right_weight.T,
        out_weight, pair_cotangent.reshape(RES, COLS, PAIR),
    )
    anywhere = pl.BlockSpec(memory_space=pl.ANY)
    pair, ag, dw = pl.pallas_call(
        write_kernel,
        out_shape=(
            jax.ShapeDtypeStruct((RES, COLS, PAIR), BF16),
            jax.ShapeDtypeStruct((2 * RES, CH), BF16),
            jax.ShapeDtypeStruct((SIZE, PAIR), F32),
        ),
        in_specs=[anywhere, anywhere, pl.BlockSpec(memory_space=pltpu.VMEM)],
        out_specs=(anywhere, anywhere, anywhere),
        scratch_shapes=[vmem((SIZE, PAIR), F32), dma((10,))],
        compiler_params=pltpu.CompilerParams(vmem_limit_bytes=60000000),
        name="write_outputs",
    )(pair, ag, fin)
    return pair.reshape(pair_cotangent.shape), ag.reshape(alignment.shape), dw


def solution(mesh):
    in_specs = (
        P("seq", "res", None),
        P("seq", "res"),
        P("res"),
        P(),
        P(),
        P(),
        P("res", None, "seq", None),
    )
    out_specs = (P("res", None, "seq", None), P("seq", "res", None), P())
    return jax.shard_map(shards, mesh=mesh, in_specs=in_specs, out_specs=out_specs, check_vma=False)
```

```python
import jax
import jax.numpy as jnp
from jax import lax
from jax.experimental import pallas as pl
from jax.experimental.pallas import tpu as pltpu
from jax.sharding import PartitionSpec as P

F32 = jnp.float32
BF16 = jnp.bfloat16
MESH = pl.DeviceIdType.MESH

NSEQ, SEQS, RES, WIDTH, CH, PAIR, COLS = 16, 32, 64, 32, 256, 128, 128
BLOCK = 8
STEPS = RES // BLOCK
EARLY = 4
SIZE = WIDTH * SEQS
NT_DIMS = (((1,), (1,)), ((), ()))


def iota(shape, dim):
    return lax.broadcasted_iota(jnp.int32, shape, dim)


def onehot(condition):
    return jnp.where(condition, 1.0, 0.0).astype(BF16)


def mm(a, b):
    return jnp.dot(a, b, preferred_element_type=F32)


def mm_nt(a, b):
    return lax.dot_general(a, b, NT_DIMS, preferred_element_type=F32)


def split(value):
    high = value.astype(BF16)
    return high, (value - high.astype(F32)).astype(BF16)


def as_column(row):
    n = row.shape[1]
    return jnp.sum(jnp.where(iota((n, n), 0) == iota((n, n), 1), row, 0.0), axis=1, keepdims=True)


def remote(src, dst, send, recv, device):
    return pltpu.make_async_remote_copy(
        src_ref=src, dst_ref=dst, send_sem=send, recv_sem=recv, device_id=device, device_id_type=MESH
    )


class Group:
    def __init__(self, count, me, device_of, source_of, slot_of, send, recv, peer_of=None):
        self.count, self.me, self.device_of = count, me, device_of
        self.peer_of = peer_of or (lambda k: (me + k) % count)
        self.source_of, self.slot_of, self.send, self.recv = source_of, slot_of, send, recv

    def each(self, body):
        if self.count <= 4:
            for k in (2, 1, 3) if self.count == 4 else (1,):
                body(k, self.peer_of(k))
        else:

            @pl.loop(0, self.count - 1)
            def _(k):
                body(k, self.peer_of(k))

    def out(self, k, other):
        return remote(
            self.source_of(other), self.slot_of(self.me), self.send.at[k], self.recv.at[self.me],
            self.device_of(other),
        )

    def start(self):
        self.each(lambda k, other: self.out(k, other).start())

    def wait(self):
        def body(k, other):
            slot = self.slot_of(other)
            remote(slot, slot, self.send.at[k], self.recv.at[other], self.device_of(other)).wait_recv()

        self.each(body)

    def sent(self):
        self.each(lambda k, other: self.out(k, other).wait_send())


def total(ref, first, count, span=slice(None)):
    value = ref[first, span].astype(F32)
    for n in range(1, count):
        value = value + ref[first + n, span].astype(F32)
    return value


def kernel(
    al_hbm, am_hbm, rm_hbm, wl_hbm, wr_hbm, w_hbm, ct_hbm,
    pair_hbm, ag_ref, fin,
    al_ref, am_ref, rm_ref, wl_ref, wr_ref, w_ref, ct_ref, in_sem,
    mask_ref, rsend, ra, rb, xr, lall,
    wf, wn, w4, lf, l2, lt, perm, rp, rm_all, rds, rt, rden, n_all, t_all, sc, rg, lgs, dw, pair_ref, pair_sem,
    wmsg, wcin, whalf, wxin, wz,
    rmsg, rcin, rhalf, rxin, rzs, rzin,
    lmsg, lx, lhalf, lz,
    c_send, c_recv,
    z_r_send, z_r_recv, z_l_send, z_l_recv, xy_r_send, xy_r_recv, x_l_send, x_l_recv,
    xy_w_send, xy_w_recv, z_w_send, z_w_recv, xy_f_send, xy_f_recv,
    xy_g_send, xy_g_recv, z_g_send, z_g_recv, x_g_send, x_g_recv, zl_g_send, zl_g_recv,
):
    a = lax.axis_index("seq")
    b = lax.axis_index("res")
    x, zh, core, y, zl = a // 4, a % 4, b % 2, b // 8, (b // 2) % 4
    xy, z = x * 4 + y, zh * 4 + zl
    z_device = lambda o: (x * 4 + o // 4, (y * 4 + o % 4) * 2 + core)
    xy_device = lambda o: ((o // 4) * 4 + zh, ((o % 4) * 4 + zl) * 2 + core)
    zh_device = lambda o: (x * 4 + o, b)
    x_device = lambda o: (o * 4 + zh, b)
    core_device = lambda o: (a, (y * 4 + zl) * 2 + o)

    def z_peer(k):
        return (z + 8 + ((k + 1) // 2) * (2 * (k % 2) - 1) + 16) % 16

    def turn(m):
        return 2 + (m * (m + 1)) // 2

    def xy_peer(k):
        return ((x + turn(k // 4)) % 4) * 4 + (y + turn(k % 4)) % 4

    def z_group(source_of, slot_of, send, recv):
        return Group(16, z, z_device, source_of, slot_of, send, recv, z_peer)

    def xy_group(source_of, slot_of, send, recv):
        return Group(16, xy, xy_device, source_of, slot_of, send, recv, xy_peer)

    def core_group(n, source_of, slot_of):
        return Group(2, core, core_device, source_of, slot_of, c_send.at[n], c_recv.at[n])

    loads = [
        pltpu.make_async_copy(src, dst, in_sem.at[n])
        for n, (src, dst) in enumerate(
            (
                (al_hbm, al_ref), (am_hbm, am_ref), (rm_hbm, rm_ref), (wl_hbm, wl_ref), (wr_hbm, wr_ref),
                (w_hbm, w_ref), (ct_hbm, ct_ref),
            )
        )
    ]
    for load in loads:
        load.start()
    barrier = pltpu.get_barrier_semaphore()

    @pl.loop(0, 15)
    def _(k):
        pl.semaphore_signal(barrier, inc=1, device_id=z_device(z_peer(k)), device_id_type=MESH)
        pl.semaphore_signal(barrier, inc=1, device_id=xy_device(xy_peer(k)), device_id_type=MESH)

    pl.semaphore_signal(barrier, inc=1, device_id=core_device(1 - core), device_id_type=MESH)
    for load in loads[:5]:
        load.wait()
    values = al_ref[...].astype(F32)
    center = values - jnp.mean(values, -1, keepdims=True)
    inverse = lax.rsqrt(jnp.mean(center * center, -1, keepdims=True) + 1e-05)
    rounded = (center * inverse).astype(BF16)
    w2 = (am_ref[...] * rm_ref[...]).astype(F32)
    row, lane = iota((128, WIDTH), 0), iota((128, WIDTH), 1)
    lanes = iota((RES, 128), 1)
    right = jnp.zeros((RES, 128), F32)
    left = jnp.zeros((32, 128), F32)
    for s in range(2):
        column = as_column(w2[s : s + 1])
        mine = rounded[s * RES : (s + 1) * RES]
        right_at = mm(onehot(row == lane + s * WIDTH), wr_ref[...]).astype(BF16)
        right = right + column * (mm_nt(mine, right_at) + jnp.where(lanes == 2 * WIDTH + s, 1.0, 0.0))
        for h in range(2):
            left_at = mm(onehot(row == lane + (2 * h + s) * WIDTH), wl_ref[...]).astype(BF16)
            span = slice(h * 32, (h + 1) * 32)
            left = left + column[span] * mm_nt(mine[span], left_at)
    r, col = iota((RES, RES), 0), iota((RES, RES), 1)
    order = onehot(col == ((r // 4) % 4) * 16 + (r // 16) * 4 + r % 4)
    right = mm(order, right.astype(BF16)).astype(BF16)
    for n in range(4):
        rsend[n] = right[n * 16 : (n + 1) * 16]
    mask_ref[...] = jnp.zeros((16, 128), F32)
    mask_ref[0:2, 0:RES] = w2
    lall[a, 0:32] = left.astype(BF16)
    lall[a, 32:48] = mask_ref[...].astype(BF16)
    loads[5].wait()
    wf[...] = w_ref[...].astype(F32)
    for d in range(WIDTH):
        piece = wf[pl.ds(d, WIDTH, stride=WIDTH), :].astype(BF16)
        wn[:, d * PAIR : (d + 1) * PAIR] = piece
        for q in range(4):
            w4[q * WIDTH : (q + 1) * WIDTH, d * PAIR : (d + 1) * PAIR] = piece
    pl.semaphore_wait(barrier, 31)
    z_r = z_group(lambda o: rsend.at[o // 4], lambda n: ra.at[n], z_r_send, z_r_recv)
    z_l = Group(
        4, zh, zh_device, lambda o: lall.at[a], lambda n: lall.at[x * 4 + n], z_l_send, z_l_recv
    )
    z_r.start()
    z_l.start()
    ra[z] = rsend[zh]
    for n in range(8):
        r, col = iota((SIZE // 8, SIZE), 0) + n * (SIZE // 8), iota((SIZE // 8, SIZE), 1)
        perm[n * (SIZE // 8) : (n + 1) * (SIZE // 8), :] = onehot(col == (r % 32) * 32 + r // 32)
    z_l.wait()
    x_l = Group(
        4, x, x_device, lambda o: lall.at[pl.ds(x * 4, 4)], lambda n: lall.at[pl.ds(n * 4, 4)],
        x_l_send, x_l_recv,
    )
    x_l.start()
    z_r.wait()

    r, col = iota((256, 256), 0), iota((256, 256), 1)
    order = onehot(col == ((r // 16) % 4) * 64 + ((r // 4) % 4) * 16 + (r // 64) * 4 + r % 4)
    moved = mm(order, ra[...].reshape(256, 128))
    lanes = iota((16, 128), 1)
    for n in range(4):
        part = [moved[n * 64 + h * 16 : n * 64 + (h + 1) * 16] for h in range(4)]
        masks = jnp.zeros((16, 128), F32)
        for h in range(4):
            own = jnp.where((lanes >= 64) & (lanes < 66), part[h], 0.0)
            masks = masks + pltpu.roll(own, (x * 8 + h * 2 + 64) % 128, 1)
        for t in range(2):
            tile = jnp.where(lanes < 64, part[2 * t], pltpu.roll(part[2 * t + 1], 64, 1))
            rb[n, t * 16 : (t + 1) * 16] = tile.astype(BF16)
        rb[n, 32:48] = masks.astype(BF16)
    xy_r = xy_group(lambda o: rb.at[o // 4], lambda n: xr.at[core, n], xy_r_send, xy_r_recv)
    xy_r.start()
    xr[core, xy] = rb[x]
    loads[6].wait()
    x_l.wait()
    blocks = lall[:, 0:32, :].reshape(NSEQ * 32, 128)
    row, lane = iota((128, 128), 0), iota((128, 128), 1)
    for h in range(2):
        for s in range(2):
            moved = mm(blocks, onehot((row == lane + (2 * h + s) * WIDTH) & (lane < WIDTH)))
            for n in range(NSEQ):
                lf[pl.ds(h * 32 * SEQS + 2 * n + s, 32, stride=SEQS), :] = moved[n * 32 : (n + 1) * 32]
    l2[...] = lf[...].astype(BF16)
    eye = onehot(iota((WIDTH, 128), 0) == iota((WIDTH, 128), 1))
    rows = BLOCK * SEQS
    for n in range(STEPS):
        lt[n] = mm_nt(eye, l2[n * rows : (n + 1) * rows, :]).astype(BF16)
    masks = lall[:, 32:48, :].astype(F32)[:, 0:8, :].reshape(128, 128).astype(BF16)
    r, col = iota((128, 128), 0), iota((128, 128), 1)
    left_mask = mm(onehot((r < SEQS) & (col == (r // 2) * 8 + r % 2)), masks).astype(BF16)
    xy_r.wait()
    c_r = core_group(0, lambda o: xr.at[core], lambda n: xr.at[n])
    c_r.start()
    def n_part(step):
        rows = BLOCK * SEQS
        l2c = l2[pl.ds(pl.multiple_of(step * rows, rows), rows), 0:WIDTH]
        for d2 in range(WIDTH // 2):
            part = mm(l2c, wn[:, d2 * 256 : (d2 + 1) * 256]).astype(BF16)
            for h in range(2):
                d = 2 * d2 + h
                for k in range(BLOCK):
                    n_all[step, d * SEQS : (d + 1) * SEQS, k * PAIR : (k + 1) * PAIR] = part[
                        k * SEQS : (k + 1) * SEQS, h * PAIR : (h + 1) * PAIR
                    ]

    pl.loop(0, EARLY)(n_part)
    c_r.wait()
    for c in range(2):
        for n in range(4):
            at = slice((c * 4 + n) * 16, (c * 4 + n + 1) * 16)
            rm_all[at] = sum(xr[c, m * 4 + n, 32:48].astype(F32) for m in range(4))
            for m in range(4):
                for t in range(2):
                    rp[at, m * 256 + t * 128 : m * 256 + (t + 1) * 128] = xr[
                        c, m * 4 + n, t * 16 : (t + 1) * 16
                    ]
    r, col = iota((128, 128), 0), iota((128, 128), 1)
    order = onehot(col == ((r // 4) % 2) * 64 + (r // 32) * 16 + ((r // 8) % 4) * 4 + r % 4)
    right_mask = mm(order, rm_all[...].astype(BF16)).astype(BF16)
    rden[...] = 1.0 / jnp.maximum(mm(right_mask, left_mask), 1.0)
    right = mm(order, rp[...]).astype(BF16)
    rds[...] = mm(right, perm[...]).astype(BF16)
    rt[...] = mm_nt(perm[...], right).astype(BF16)

    def scale_of(step):
        return pltpu.roll(rden[...], lax.rem(128 - step * BLOCK, 128), 1)
    dw[...] = jnp.zeros_like(dw)

    @pl.loop(0, STEPS)
    def _(step):
        scale = scale_of(step)
        for k in range(BLOCK):
            sc[step, :, k * PAIR : (k + 1) * PAIR] = (
                ct_ref[step * BLOCK + k].astype(F32) * scale[:, k : k + 1]
            ).astype(BF16)
        for k2 in range(BLOCK // 2):
            part = mm(rt[...], sc[step, :, k2 * 256 : (k2 + 1) * 256]).astype(BF16)
            for h in range(2):
                k = 2 * k2 + h
                for d in range(WIDTH):
                    t_all[step, k * SEQS : (k + 1) * SEQS, d * PAIR : (d + 1) * PAIR] = part[
                        d * SEQS : (d + 1) * SEQS, h * PAIR : (h + 1) * PAIR
                    ]
        dw[...] += mm(lt[step], t_all[step])
    for c in range(2):
        for n in range(16):
            d = c * 16 + n
            wmsg[c, n] = dw[:, d * PAIR : (d + 1) * PAIR].astype(BF16)
    c_w = core_group(1, lambda o: wmsg.at[o], lambda n: wcin)
    c_w.start()
    rg[...] = jnp.zeros_like(rg)

    def right_part(step):
        rg[...] += mm_nt(sc[step], n_all[step])

    pl.loop(0, EARLY)(right_part)
    c_w.wait()
    for n in range(16):
        whalf[n] = (wmsg[core, n].astype(F32) + wcin[n].astype(F32)).astype(BF16)
    xy_w = xy_group(lambda o: whalf.at[o], lambda n: wxin.at[n], xy_w_send, xy_w_recv)
    xy_w.start()
    wxin[xy] = whalf[xy]
    @pl.loop(EARLY, STEPS)
    def _(step):
        n_part(step)
        right_part(step)
    grads = mm(rg[...].astype(BF16), perm[...]).astype(BF16)
    r, col = iota((128, 128), 0), iota((128, 128), 1)
    order = onehot(col == ((r // 16) % 4) * 32 + ((r // 4) % 4) * 8 + (r // 64) * 4 + r % 4)
    grads = mm(order, grads).astype(BF16)
    for c in range(2):
        for m in range(4):
            for n in range(4):
                at = slice((c * 4 + n) * 16, (c * 4 + n + 1) * 16)
                for t in range(2):
                    rmsg[c, m * 4 + n, t * 16 : (t + 1) * 16] = grads[
                        at, m * 256 + t * 128 : m * 256 + (t + 1) * 128
                    ]
    c_g = core_group(2, lambda o: rmsg.at[o], lambda n: rcin)
    c_g.start()
    xy_w.wait()
    wz[z] = total(wxin, 0, 16).astype(BF16)
    z_w = z_group(lambda o: wz.at[z], lambda n: wz.at[n], z_w_send, z_w_recv)
    z_w.start()
    def left_part(step):
        rows = BLOCK * SEQS
        lgs[pl.ds(pl.multiple_of(step * rows, rows), rows), :] = mm_nt(t_all[step], w4[...])

    pl.loop(0, 4)(left_part)
    c_g.wait()
    for n in range(16):
        rhalf[n] = (rmsg[core, n].astype(F32) + rcin[n].astype(F32)).astype(BF16)
    xy_g = xy_group(lambda o: rhalf.at[o], lambda n: rxin.at[n], xy_g_send, xy_g_recv)
    xy_g.start()
    rxin[xy] = rhalf[xy]
    pl.loop(4, STEPS)(left_part)
    lane = iota((32, 128), 1) // WIDTH
    for n in range(NSEQ):
        out = lgs[pl.ds(2 * n, 32, stride=SEQS), :]
        for q in range(1, 4):
            piece = lgs[pl.ds((q // 2) * 32 * SEQS + 2 * n + q % 2, 32, stride=SEQS), :]
            out = jnp.where(lane == q, piece, out)
        lmsg[n] = out.astype(BF16)
    x_g = Group(
        4, x, x_device, lambda o: lmsg.at[pl.ds(o * 4, 4)], lambda n: lx.at[n], x_g_send, x_g_recv
    )
    x_g.start()
    lx[x] = lmsg[pl.ds(x * 4, 4)]
    def pair_part(step):
        scale = scale_of(step)
        for k2 in range(BLOCK // 2):
            part = mm(rds[...], n_all[step, :, k2 * 256 : (k2 + 1) * 256])
            for h in range(2):
                k = 2 * k2 + h
                pair_ref[step * BLOCK + k] = (
                    part[:, h * PAIR : (h + 1) * PAIR] * scale[:, k : k + 1]
                ).astype(BF16)

    def pair_copy(n):
        span = pl.ds(n * (RES // 2), RES // 2)
        return pltpu.make_async_copy(pair_ref.at[span], pair_hbm.at[span], pair_sem.at[n])

    pl.loop(0, 4)(pair_part)
    pair_copy(0).start()
    xy_g.wait()
    sums = [total(rxin, m * 4, 4).astype(BF16) for m in range(4)]
    r, col = iota((64, 64), 0), iota((64, 64), 1)
    order = onehot(col == ((r // 4) % 4) * 16 + (r // 16) * 4 + r % 4)
    for t in range(2):
        moved = mm(order, jnp.concatenate([v[t * 16 : (t + 1) * 16] for v in sums], axis=0))
        for h in range(2):
            own = moved if h == 0 else pltpu.roll(moved, 64, 1)
            for n in range(4):
                rzs[(2 * t + h) * 4 + n] = own[n * 16 : (n + 1) * 16].astype(BF16)
    z_g = z_group(lambda o: rzs.at[o], lambda n: rzin.at[n], z_g_send, z_g_recv)
    z_g.start()
    rzin[z] = rzs[z]
    x_g.wait()
    lhalf[...] = total(lx, 0, 4).astype(BF16)
    zl_g = Group(4, zh, zh_device, lambda o: lhalf.at[o], lambda n: lz.at[n], zl_g_send, zl_g_recv)
    zl_g.start()
    lz[zh] = lhalf[zh]
    z_w.wait()
    fin[core, xy] = total(wz, 0, 16).astype(BF16)
    xy_f = xy_group(lambda o: fin.at[core, xy], lambda n: fin.at[core, n], xy_f_send, xy_f_recv)
    xy_f.start()
    pl.loop(4, STEPS)(pair_part)
    pair_copy(1).start()
    values = al_ref[...].astype(F32)
    center = values - jnp.mean(values, -1, keepdims=True)
    inverse = lax.rsqrt(jnp.mean(center * center, -1, keepdims=True) + 1e-05)
    normal = center * inverse
    w2 = (am_ref[...] * rm_ref[...]).astype(F32)
    zl_g.wait()
    left = split(total(lz, 0, 4))
    z_g.wait()
    r, col = iota((RES, RES), 0), iota((RES, RES), 1)
    order = onehot(col == ((r // 4) % 4) * 16 + (r // 16) * 4 + r % 4)
    right = split(jnp.concatenate([total(rzin, n * 4, 4) for n in range(4)], axis=0))
    right = [mm(order, v).astype(BF16) for v in right]
    row, lane = iota((128, WIDTH), 0), iota((128, WIDTH), 1)
    for s in range(2):
        right_at = mm(onehot(row == lane + s * WIDTH), wr_ref[...]).astype(BF16)
        parts = []
        for h in range(2):
            left_at = mm(onehot(row == lane + (2 * h + s) * WIDTH), wl_ref[...]).astype(BF16)
            parts.append(mm(left[0], left_at) + mm(left[1], left_at))
        grad = jnp.concatenate(parts, axis=0) + mm(right[0], right_at) + mm(right[1], right_at)
        grad = grad * as_column(w2[s : s + 1])
        span = slice(s * RES, (s + 1) * RES)
        first = jnp.mean(grad, -1, keepdims=True)
        second = jnp.mean(grad * normal[span], -1, keepdims=True)
        ag_ref[span] = (inverse[span] * (grad - first - normal[span] * second)).astype(BF16)
    xy_f.wait()
    c_f = core_group(3, lambda o: fin.at[core], lambda n: fin.at[n])
    c_f.start()
    for group in (z_r, z_l, xy_r, x_l, c_r, c_w, c_g, xy_w, z_w, xy_f, xy_g, z_g, x_g, zl_g, c_f):
        group.sent()
    for n in range(2):
        pair_copy(n).wait()
    c_f.wait()


def write_kernel(pair_in, ag_in, fin_in, pair_out, ag_out, dw_out, pair_ref, ag_ref, fin_ref, dw_ref, sem, out_sem):
    count = 8
    rows = RES // count
    ins = [
        pltpu.make_async_copy(fin_in, fin_ref, sem.at[0]),
        pltpu.make_async_copy(ag_in, ag_ref, sem.at[1]),
    ]
    outs = [
        pltpu.make_async_copy(dw_ref, dw_out, out_sem.at[0]),
        pltpu.make_async_copy(ag_ref, ag_out, out_sem.at[1]),
    ]
    for n in range(count):
        span = pl.ds(n * rows, rows)
        ins.append(pltpu.make_async_copy(pair_in.at[span], pair_ref.at[span], sem.at[2 + n]))
        outs.append(pltpu.make_async_copy(pair_ref.at[span], pair_out.at[span], out_sem.at[2 + n]))
    for copy in ins:
        copy.start()
    for n, copy in enumerate(ins):
        copy.wait()
        if n == 0:
            for c in range(2):
                for d in range(16):
                    dw_ref[pl.ds(c * 16 + d, WIDTH, stride=WIDTH), :] = fin_ref[c, d].astype(F32)
        outs[n].start()
    for copy in outs:
        copy.wait()


def shards(alignment, align_mask, residue_mask, left_weight, right_weight, out_weight, pair_cotangent):
    dma = pltpu.SemaphoreType.DMA
    vmem = pltpu.VMEM
    pair, ag, fin = pl.pallas_call(
        kernel,
        out_shape=(
            jax.ShapeDtypeStruct((RES, COLS, PAIR), BF16),
            jax.ShapeDtypeStruct((2 * RES, CH), BF16),
            jax.ShapeDtypeStruct((2, 16, WIDTH, PAIR), BF16),
        ),
        in_specs=[pl.BlockSpec(memory_space=pltpu.HBM)] * 7,
        out_specs=(pl.BlockSpec(memory_space=pl.ANY),) + (pl.BlockSpec(memory_space=pltpu.VMEM),) * 2,
        scratch_shapes=[
            vmem((2 * RES, CH), BF16), vmem((2, RES), jnp.int32), vmem((1, RES), jnp.int32),
            vmem((WIDTH, CH), BF16), vmem((WIDTH, CH), BF16), vmem((SIZE, PAIR), BF16),
            vmem((RES, COLS, PAIR), BF16), dma((7,)),
            vmem((16, 128), F32), vmem((4, 16, 128), BF16), vmem((16, 16, 128), BF16),
            vmem((4, 48, 128), BF16), vmem((2, 16, 48, 128), BF16), vmem((NSEQ, 48, 128), BF16),
            vmem((SIZE, PAIR), F32), vmem((WIDTH, WIDTH * PAIR), BF16), vmem((128, WIDTH * PAIR), BF16),
            vmem((RES * SEQS, 128), F32), vmem((RES * SEQS, 128), BF16),
            vmem((STEPS, WIDTH, BLOCK * SEQS), BF16), vmem((SIZE, SIZE), BF16),
            vmem((COLS, SIZE), BF16), vmem((COLS, 128), F32), vmem((COLS, SIZE), BF16),
            vmem((SIZE, COLS), BF16), vmem((COLS, 128), F32),
            vmem((STEPS, SIZE, BLOCK * PAIR), BF16), vmem((STEPS, BLOCK * SEQS, WIDTH * PAIR), BF16),
            vmem((STEPS, COLS, BLOCK * PAIR), BF16), vmem((COLS, SIZE), F32),
            vmem((RES * SEQS, 128), F32), vmem((WIDTH, WIDTH * PAIR), F32),
            vmem((RES, COLS, PAIR), BF16), dma((2,)),
            vmem((2, 16, 32, 128), BF16), vmem((16, 32, 128), BF16), vmem((16, 32, 128), BF16),
            vmem((16, 32, 128), BF16), vmem((16, 32, 128), BF16),
            vmem((2, 16, 32, 128), BF16), vmem((16, 32, 128), BF16), vmem((16, 32, 128), BF16),
            vmem((16, 32, 128), BF16), vmem((16, 16, 128), BF16), vmem((16, 16, 128), BF16),
            vmem((NSEQ, 32, 128), BF16), vmem((4, 4, 32, 128), BF16), vmem((4, 32, 128), BF16),
            vmem((4, 32, 128), BF16),
            dma((4, 2)), dma((4, 2)),
            dma((16,)), dma((16,)), dma((4,)), dma((4,)), dma((16,)), dma((16,)), dma((4,)), dma((4,)),
            dma((16,)), dma((16,)), dma((16,)), dma((16,)), dma((16,)), dma((16,)),
            dma((16,)), dma((16,)), dma((16,)), dma((16,)), dma((4,)), dma((4,)), dma((4,)), dma((4,)),
        ],
        compiler_params=pltpu.CompilerParams(
            collective_id=0, has_side_effects=True, vmem_limit_bytes=60000000
        ),
        name="pair_update",
    )(
        alignment.reshape(2 * RES, CH), align_mask, residue_mask.reshape(1, RES), left_weight.T, right_weight.T,
        out_weight, pair_cotangent.reshape(RES, COLS, PAIR),
    )
    anywhere = pl.BlockSpec(memory_space=pl.ANY)
    pair, ag, dw = pl.pallas_call(
        write_kernel,
        out_shape=(
            jax.ShapeDtypeStruct((RES, COLS, PAIR), BF16),
            jax.ShapeDtypeStruct((2 * RES, CH), BF16),
            jax.ShapeDtypeStruct((SIZE, PAIR), F32),
        ),
        in_specs=[anywhere] * 3,
        out_specs=(anywhere, anywhere, anywhere),
        scratch_shapes=[
            vmem((RES, COLS, PAIR), BF16), vmem((2 * RES, CH), BF16), vmem((2, 16, WIDTH, PAIR), BF16),
            vmem((SIZE, PAIR), F32), dma((10,)), dma((10,)),
        ],
        compiler_params=pltpu.CompilerParams(vmem_limit_bytes=60000000),
        name="write_outputs",
    )(pair, ag, fin)
    return pair.reshape(pair_cotangent.shape), ag.reshape(alignment.shape), dw


def solution(mesh):
    in_specs = (
        P("seq", "res", None),
        P("seq", "res"),
        P("res"),
        P(),
        P(),
        P(),
        P("res", None, "seq", None),
    )
    out_specs = (P("res", None, "seq", None), P("seq", "res", None), P())
    return jax.shard_map(shards, mesh=mesh, in_specs=in_specs, out_specs=out_specs, check_vma=False)
```

```python
import jax
import jax.numpy as jnp
from jax import lax
from jax.experimental import pallas as pl
from jax.experimental.pallas import tpu as pltpu
from jax.sharding import PartitionSpec as P

F32 = jnp.float32
BF16 = jnp.bfloat16
MESH = pl.DeviceIdType.MESH

NSEQ, SEQS, RES, WIDTH, CH, PAIR, COLS = 16, 32, 64, 32, 256, 128, 128
BLOCK = 8
STEPS = RES // BLOCK
EARLY = 4
SIZE = WIDTH * SEQS
NT_DIMS = (((1,), (1,)), ((), ()))


def iota(shape, dim):
    return lax.broadcasted_iota(jnp.int32, shape, dim)


def onehot(condition):
    return jnp.where(condition, 1.0, 0.0).astype(BF16)


def mm(a, b):
    return jnp.dot(a, b, preferred_element_type=F32)


def mm_nt(a, b):
    return lax.dot_general(a, b, NT_DIMS, preferred_element_type=F32)


def split(value):
    high = value.astype(BF16)
    return high, (value - high.astype(F32)).astype(BF16)


def as_column(row):
    n = row.shape[1]
    return jnp.sum(jnp.where(iota((n, n), 0) == iota((n, n), 1), row, 0.0), axis=1, keepdims=True)


def remote(src, dst, send, recv, device):
    return pltpu.make_async_remote_copy(
        src_ref=src, dst_ref=dst, send_sem=send, recv_sem=recv, device_id=device, device_id_type=MESH
    )


class Group:
    def __init__(self, count, me, device_of, source_of, slot_of, send, recv, peer_of=None):
        self.count, self.me, self.device_of = count, me, device_of
        self.peer_of = peer_of or (lambda k: (me + k) % count)
        self.source_of, self.slot_of, self.send, self.recv = source_of, slot_of, send, recv

    def each(self, body):
        if self.count <= 4:
            for k in (2, 1, 3) if self.count == 4 else (1,):
                body(k, self.peer_of(k))
        else:

            @pl.loop(0, self.count - 1)
            def _(k):
                body(k, self.peer_of(k))

    def out(self, k, other):
        return remote(
            self.source_of(other), self.slot_of(self.me), self.send.at[k], self.recv.at[self.me],
            self.device_of(other),
        )

    def start(self):
        self.each(lambda k, other: self.out(k, other).start())

    def wait(self):
        def body(k, other):
            slot = self.slot_of(other)
            remote(slot, slot, self.send.at[k], self.recv.at[other], self.device_of(other)).wait_recv()

        self.each(body)

    def sent(self):
        self.each(lambda k, other: self.out(k, other).wait_send())


def total(ref, first, count, span=slice(None)):
    value = ref[first, span].astype(F32)
    for n in range(1, count):
        value = value + ref[first + n, span].astype(F32)
    return value


def kernel(
    al_hbm, am_hbm, rm_hbm, wl_hbm, wr_hbm, w_hbm, ct_hbm,
    pair_hbm, ag_ref, fin,
    al_ref, am_ref, rm_ref, wl_ref, wr_ref, w_ref, ct_ref, in_sem,
    mask_ref, rsend, ra, rb, xr, lall,
    wf, wn, w4, lf, l2, lt, perm, rp, rm_all, rds, rt, rden, n_all, t_all, sc, rg, lgs, dw, pair_ref, pair_sem,
    wmsg, wcin, whalf, wxin, wz,
    rmsg, rcin, rhalf, rxin, rzs, rzin,
    lmsg, lx, lhalf, lz,
    c_send, c_recv,
    z_r_send, z_r_recv, z_l_send, z_l_recv, xy_r_send, xy_r_recv, x_l_send, x_l_recv,
    xy_w_send, xy_w_recv, z_w_send, z_w_recv, xy_f_send, xy_f_recv,
    xy_g_send, xy_g_recv, z_g_send, z_g_recv, x_g_send, x_g_recv, zl_g_send, zl_g_recv,
):
    a = lax.axis_index("seq")
    b = lax.axis_index("res")
    x, zh, core, y, zl = a // 4, a % 4, b % 2, b // 8, (b // 2) % 4
    xy, z = x * 4 + y, zh * 4 + zl
    z_device = lambda o: (x * 4 + o // 4, (y * 4 + o % 4) * 2 + core)
    xy_device = lambda o: ((o // 4) * 4 + zh, ((o % 4) * 4 + zl) * 2 + core)
    zh_device = lambda o: (x * 4 + o, b)
    x_device = lambda o: (o * 4 + zh, b)
    core_device = lambda o: (a, (y * 4 + zl) * 2 + o)

    def z_peer(k):
        return (z + 8 + ((k + 1) // 2) * (2 * (k % 2) - 1) + 16) % 16

    def turn(m):
        return 2 + (m * (m + 1)) // 2

    def xy_peer(k):
        return ((x + turn(k // 4)) % 4) * 4 + (y + turn(k % 4)) % 4

    def z_group(source_of, slot_of, send, recv):
        return Group(16, z, z_device, source_of, slot_of, send, recv, z_peer)

    def xy_group(source_of, slot_of, send, recv):
        return Group(16, xy, xy_device, source_of, slot_of, send, recv, xy_peer)

    def core_group(n, source_of, slot_of):
        return Group(2, core, core_device, source_of, slot_of, c_send.at[n], c_recv.at[n])

    loads = [
        pltpu.make_async_copy(src, dst, in_sem.at[n])
        for n, (src, dst) in enumerate(
            (
                (al_hbm, al_ref), (am_hbm, am_ref), (rm_hbm, rm_ref), (wl_hbm, wl_ref), (wr_hbm, wr_ref),
                (w_hbm, w_ref), (ct_hbm, ct_ref),
            )
        )
    ]
    barrier = pltpu.get_barrier_semaphore()

    @pl.loop(0, 15)
    def _(k):
        pl.semaphore_signal(barrier, inc=1, device_id=z_device(z_peer(k)), device_id_type=MESH)
        pl.semaphore_signal(barrier, inc=1, device_id=xy_device(xy_peer(k)), device_id_type=MESH)

    pl.semaphore_signal(barrier, inc=1, device_id=core_device(1 - core), device_id_type=MESH)
    for load in loads:
        load.start()
    for load in loads[:5]:
        load.wait()
    values = al_ref[...].astype(F32)
    center = values - jnp.mean(values, -1, keepdims=True)
    inverse = lax.rsqrt(jnp.mean(center * center, -1, keepdims=True) + 1e-05)
    rounded = (center * inverse).astype(BF16)
    w2 = (am_ref[...] * rm_ref[...]).astype(F32)
    row, lane = iota((128, WIDTH), 0), iota((128, WIDTH), 1)
    lanes = iota((RES, 128), 1)
    right = jnp.zeros((RES, 128), F32)
    left = jnp.zeros((32, 128), F32)
    for s in range(2):
        column = as_column(w2[s : s + 1])
        mine = rounded[s * RES : (s + 1) * RES]
        right_at = mm(onehot(row == lane + s * WIDTH), wr_ref[...]).astype(BF16)
        right = right + column * (mm_nt(mine, right_at) + jnp.where(lanes == 2 * WIDTH + s, 1.0, 0.0))
        for h in range(2):
            left_at = mm(onehot(row == lane + (2 * h + s) * WIDTH), wl_ref[...]).astype(BF16)
            span = slice(h * 32, (h + 1) * 32)
            left = left + column[span] * mm_nt(mine[span], left_at)
    r, col = iota((RES, RES), 0), iota((RES, RES), 1)
    order = onehot(col == ((r // 4) % 4) * 16 + (r // 16) * 4 + r % 4)
    right = mm(order, right.astype(BF16)).astype(BF16)
    for n in range(4):
        rsend[n] = right[n * 16 : (n + 1) * 16]
    mask_ref[...] = jnp.zeros((16, 128), F32)
    mask_ref[0:2, 0:RES] = w2
    lall[a, 0:32] = left.astype(BF16)
    lall[a, 32:48] = mask_ref[...].astype(BF16)
    loads[5].wait()
    wf[...] = w_ref[...].astype(F32)
    for d in range(WIDTH):
        piece = wf[pl.ds(d, WIDTH, stride=WIDTH), :].astype(BF16)
        wn[:, d * PAIR : (d + 1) * PAIR] = piece
        for q in range(4):
            w4[q * WIDTH : (q + 1) * WIDTH, d * PAIR : (d + 1) * PAIR] = piece
    pl.semaphore_wait(barrier, 31)
    z_r = z_group(lambda o: rsend.at[o // 4], lambda n: ra.at[n], z_r_send, z_r_recv)
    z_l = Group(
        4, zh, zh_device, lambda o: lall.at[a], lambda n: lall.at[x * 4 + n], z_l_send, z_l_recv
    )
    z_r.start()
    z_l.start()
    ra[z] = rsend[zh]
    for n in range(8):
        r, col = iota((SIZE // 8, SIZE), 0) + n * (SIZE // 8), iota((SIZE // 8, SIZE), 1)
        perm[n * (SIZE // 8) : (n + 1) * (SIZE // 8), :] = onehot(col == (r % 32) * 32 + r // 32)
    z_l.wait()
    x_l = Group(
        4, x, x_device, lambda o: lall.at[pl.ds(x * 4, 4)], lambda n: lall.at[pl.ds(n * 4, 4)],
        x_l_send, x_l_recv,
    )
    x_l.start()
    z_r.wait()

    r, col = iota((256, 256), 0), iota((256, 256), 1)
    order = onehot(col == ((r // 16) % 4) * 64 + ((r // 4) % 4) * 16 + (r // 64) * 4 + r % 4)
    moved = mm(order, ra[...].reshape(256, 128))
    lanes = iota((16, 128), 1)
    for n in range(4):
        part = [moved[n * 64 + h * 16 : n * 64 + (h + 1) * 16] for h in range(4)]
        masks = jnp.zeros((16, 128), F32)
        for h in range(4):
            own = jnp.where((lanes >= 64) & (lanes < 66), part[h], 0.0)
            masks = masks + pltpu.roll(own, (x * 8 + h * 2 + 64) % 128, 1)
        for t in range(2):
            tile = jnp.where(lanes < 64, part[2 * t], pltpu.roll(part[2 * t + 1], 64, 1))
            rb[n, t * 16 : (t + 1) * 16] = tile.astype(BF16)
        rb[n, 32:48] = masks.astype(BF16)
    xy_r = xy_group(lambda o: rb.at[o // 4], lambda n: xr.at[core, n], xy_r_send, xy_r_recv)
    xy_r.start()
    xr[core, xy] = rb[x]
    loads[6].wait()
    x_l.wait()
    blocks = lall[:, 0:32, :].reshape(NSEQ * 32, 128)
    row, lane = iota((128, 128), 0), iota((128, 128), 1)
    for h in range(2):
        for s in range(2):
            moved = mm(blocks, onehot((row == lane + (2 * h + s) * WIDTH) & (lane < WIDTH)))
            for n in range(NSEQ):
                lf[pl.ds(h * 32 * SEQS + 2 * n + s, 32, stride=SEQS), :] = moved[n * 32 : (n + 1) * 32]
    l2[...] = lf[...].astype(BF16)
    eye = onehot(iota((WIDTH, 128), 0) == iota((WIDTH, 128), 1))
    rows = BLOCK * SEQS
    for n in range(STEPS):
        lt[n] = mm_nt(eye, l2[n * rows : (n + 1) * rows, :]).astype(BF16)
    masks = lall[:, 32:48, :].astype(F32)[:, 0:8, :].reshape(128, 128).astype(BF16)
    r, col = iota((128, 128), 0), iota((128, 128), 1)
    left_mask = mm(onehot((r < SEQS) & (col == (r // 2) * 8 + r % 2)), masks).astype(BF16)
    xy_r.wait()
    c_r = core_group(0, lambda o: xr.at[core], lambda n: xr.at[n])
    c_r.start()
    def n_part(step):
        l2c = l2[step * rows : (step + 1) * rows, 0:WIDTH]
        for d2 in range(WIDTH // 2):
            part = mm(l2c, wn[:, d2 * 256 : (d2 + 1) * 256]).astype(BF16)
            for h in range(2):
                d = 2 * d2 + h
                for k in range(BLOCK):
                    n_all[step, d * SEQS : (d + 1) * SEQS, k * PAIR : (k + 1) * PAIR] = part[
                        k * SEQS : (k + 1) * SEQS, h * PAIR : (h + 1) * PAIR
                    ]

    for step in range(EARLY):
        n_part(step)
    c_r.wait()
    for c in range(2):
        for n in range(4):
            at = slice((c * 4 + n) * 16, (c * 4 + n + 1) * 16)
            rm_all[at] = sum(xr[c, m * 4 + n, 32:48].astype(F32) for m in range(4))
            for m in range(4):
                for t in range(2):
                    rp[at, m * 256 + t * 128 : m * 256 + (t + 1) * 128] = xr[
                        c, m * 4 + n, t * 16 : (t + 1) * 16
                    ]
    r, col = iota((128, 128), 0), iota((128, 128), 1)
    order = onehot(col == ((r // 4) % 2) * 64 + (r // 32) * 16 + ((r // 8) % 4) * 4 + r % 4)
    right_mask = mm(order, rm_all[...].astype(BF16)).astype(BF16)
    rden[...] = 1.0 / jnp.maximum(mm(right_mask, left_mask), 1.0)
    right = mm(order, rp[...]).astype(BF16)
    rds[...] = mm(right, perm[...]).astype(BF16)
    rt[...] = mm_nt(perm[...], right).astype(BF16)

    def scale_of(step):
        return pltpu.roll(rden[...], (128 - step * BLOCK) % 128, 1)
    dw[...] = jnp.zeros_like(dw)

    def t_part(step):
        scale = scale_of(step)
        for k in range(BLOCK):
            sc[step, :, k * PAIR : (k + 1) * PAIR] = (
                ct_ref[step * BLOCK + k].astype(F32) * scale[:, k : k + 1]
            ).astype(BF16)
        for k2 in range(BLOCK // 2):
            part = mm(rt[...], sc[step, :, k2 * 256 : (k2 + 1) * 256]).astype(BF16)
            for h in range(2):
                k = 2 * k2 + h
                for d in range(WIDTH):
                    t_all[step, k * SEQS : (k + 1) * SEQS, d * PAIR : (d + 1) * PAIR] = part[
                        d * SEQS : (d + 1) * SEQS, h * PAIR : (h + 1) * PAIR
                    ]

    for step in range(STEPS + 1):
        if step < STEPS:
            t_part(step)
        if step > 0:
            dw[...] += mm(lt[step - 1], t_all[step - 1])
    for c in range(2):
        for n in range(16):
            d = c * 16 + n
            wmsg[c, n] = dw[:, d * PAIR : (d + 1) * PAIR].astype(BF16)
    c_w = core_group(1, lambda o: wmsg.at[o], lambda n: wcin)
    c_w.start()
    rg[...] = jnp.zeros_like(rg)

    def right_part(step):
        rg[...] += mm_nt(n_all[step], sc[step])

    for step in range(EARLY):
        right_part(step)
    c_w.wait()
    for n in range(16):
        whalf[n] = (wmsg[core, n].astype(F32) + wcin[n].astype(F32)).astype(BF16)
    xy_w = xy_group(lambda o: whalf.at[o], lambda n: wxin.at[n], xy_w_send, xy_w_recv)
    xy_w.start()
    wxin[xy] = whalf[xy]
    for step in range(EARLY, STEPS):
        n_part(step)
    for step in range(EARLY, STEPS):
        right_part(step)
    r, col = iota((128, 128), 0), iota((128, 128), 1)
    order = onehot(col == ((r // 16) % 4) * 32 + ((r // 4) % 4) * 8 + (r // 64) * 4 + r % 4)
    grads = mm_nt(order, rg[...].astype(BF16)).astype(BF16)
    grads = mm(grads, perm[...]).astype(BF16)
    for c in range(2):
        for m in range(4):
            for n in range(4):
                at = slice((c * 4 + n) * 16, (c * 4 + n + 1) * 16)
                for t in range(2):
                    rmsg[c, m * 4 + n, t * 16 : (t + 1) * 16] = grads[
                        at, m * 256 + t * 128 : m * 256 + (t + 1) * 128
                    ]
    c_g = core_group(2, lambda o: rmsg.at[o], lambda n: rcin)
    c_g.start()
    xy_w.wait()
    wz[z] = total(wxin, 0, 16).astype(BF16)
    z_w = z_group(lambda o: wz.at[z], lambda n: wz.at[n], z_w_send, z_w_recv)
    z_w.start()
    def left_part(n):
        blocks = t_all[2 * n : 2 * n + 2].reshape(2 * rows, WIDTH * PAIR)
        lgs[n * 2 * rows : (n + 1) * 2 * rows, :] = mm_nt(blocks, w4[...])

    left_part(0)
    c_g.wait()
    for n in range(16):
        rhalf[n] = (rmsg[core, n].astype(F32) + rcin[n].astype(F32)).astype(BF16)
    xy_g = xy_group(lambda o: rhalf.at[o], lambda n: rxin.at[n], xy_g_send, xy_g_recv)
    xy_g.start()
    rxin[xy] = rhalf[xy]
    for n in range(1, STEPS // 2):
        left_part(n)
    lane = iota((32, 128), 1) // WIDTH
    for n in range(NSEQ):
        out = lgs[pl.ds(2 * n, 32, stride=SEQS), :]
        for q in range(1, 4):
            piece = lgs[pl.ds((q // 2) * 32 * SEQS + 2 * n + q % 2, 32, stride=SEQS), :]
            out = jnp.where(lane == q, piece, out)
        lmsg[n] = out.astype(BF16)
    x_g = Group(
        4, x, x_device, lambda o: lmsg.at[pl.ds(o * 4, 4)], lambda n: lx.at[n], x_g_send, x_g_recv
    )
    x_g.start()
    lx[x] = lmsg[pl.ds(x * 4, 4)]
    def pair_part(step):
        scale = scale_of(step)
        for k2 in range(BLOCK // 2):
            part = mm(rds[...], n_all[step, :, k2 * 256 : (k2 + 1) * 256])
            for h in range(2):
                k = 2 * k2 + h
                pair_ref[step * BLOCK + k] = (
                    part[:, h * PAIR : (h + 1) * PAIR] * scale[:, k : k + 1]
                ).astype(BF16)

    def pair_copy(n):
        span = pl.ds(n * (RES // 2), RES // 2)
        return pltpu.make_async_copy(pair_ref.at[span], pair_hbm.at[span], pair_sem.at[n])

    for step in range(STEPS):
        pair_part(step)
        if step == STEPS // 2 - 1:
            pair_copy(0).start()
    pair_copy(1).start()
    xy_g.wait()
    sums = [total(rxin, m * 4, 4).astype(BF16) for m in range(4)]
    r, col = iota((64, 64), 0), iota((64, 64), 1)
    order = onehot(col == ((r // 4) % 4) * 16 + (r // 16) * 4 + r % 4)
    for t in range(2):
        moved = mm(order, jnp.concatenate([v[t * 16 : (t + 1) * 16] for v in sums], axis=0))
        for h in range(2):
            own = moved if h == 0 else pltpu.roll(moved, 64, 1)
            for n in range(4):
                rzs[(2 * t + h) * 4 + n] = own[n * 16 : (n + 1) * 16].astype(BF16)
    z_g = z_group(lambda o: rzs.at[o], lambda n: rzin.at[n], z_g_send, z_g_recv)
    z_g.start()
    rzin[z] = rzs[z]
    x_g.wait()
    lhalf[...] = total(lx, 0, 4).astype(BF16)
    zl_g = Group(4, zh, zh_device, lambda o: lhalf.at[o], lambda n: lz.at[n], zl_g_send, zl_g_recv)
    zl_g.start()
    lz[zh] = lhalf[zh]
    z_w.wait()
    fin[core, xy] = total(wz, 0, 16).astype(BF16)
    xy_f = xy_group(lambda o: fin.at[core, xy], lambda n: fin.at[core, n], xy_f_send, xy_f_recv)
    xy_f.start()
    values = al_ref[...].astype(F32)
    center = values - jnp.mean(values, -1, keepdims=True)
    inverse = lax.rsqrt(jnp.mean(center * center, -1, keepdims=True) + 1e-05)
    normal = center * inverse
    w2 = (am_ref[...] * rm_ref[...]).astype(F32)
    zl_g.wait()
    left = split(total(lz, 0, 4))
    z_g.wait()
    r, col = iota((RES, RES), 0), iota((RES, RES), 1)
    order = onehot(col == ((r // 4) % 4) * 16 + (r // 16) * 4 + r % 4)
    right = split(jnp.concatenate([total(rzin, n * 4, 4) for n in range(4)], axis=0))
    right = [mm(order, v).astype(BF16) for v in right]
    row, lane = iota((128, WIDTH), 0), iota((128, WIDTH), 1)
    for s in range(2):
        right_at = mm(onehot(row == lane + s * WIDTH), wr_ref[...]).astype(BF16)
        parts = []
        for h in range(2):
            left_at = mm(onehot(row == lane + (2 * h + s) * WIDTH), wl_ref[...]).astype(BF16)
            parts.append(mm(left[0], left_at) + mm(left[1], left_at))
        grad = jnp.concatenate(parts, axis=0) + mm(right[0], right_at) + mm(right[1], right_at)
        grad = grad * as_column(w2[s : s + 1])
        span = slice(s * RES, (s + 1) * RES)
        first = jnp.mean(grad, -1, keepdims=True)
        second = jnp.mean(grad * normal[span], -1, keepdims=True)
        ag_ref[span] = (inverse[span] * (grad - first - normal[span] * second)).astype(BF16)
    xy_f.wait()
    c_f = core_group(3, lambda o: fin.at[core], lambda n: fin.at[n])
    c_f.start()
    for group in (z_r, z_l, xy_r, x_l, c_r, c_w, c_g, xy_w, z_w, xy_f, xy_g, z_g, x_g, zl_g, c_f):
        group.sent()
    for n in range(2):
        pair_copy(n).wait()
    c_f.wait()


def write_kernel(pair_in, ag_in, fin_in, pair_out, ag_out, dw_out, pair_ref, ag_ref, fin_ref, dw_ref, sem, out_sem):
    count = 8
    rows = RES // count
    ins = [
        pltpu.make_async_copy(fin_in, fin_ref, sem.at[0]),
        pltpu.make_async_copy(ag_in, ag_ref, sem.at[1]),
    ]
    outs = [
        pltpu.make_async_copy(dw_ref, dw_out, out_sem.at[0]),
        pltpu.make_async_copy(ag_ref, ag_out, out_sem.at[1]),
    ]
    for n in range(count):
        span = pl.ds(n * rows, rows)
        ins.append(pltpu.make_async_copy(pair_in.at[span], pair_ref.at[span], sem.at[2 + n]))
        outs.append(pltpu.make_async_copy(pair_ref.at[span], pair_out.at[span], out_sem.at[2 + n]))
    for copy in ins:
        copy.start()
    for n, copy in enumerate(ins):
        copy.wait()
        if n == 0:
            for c in range(2):
                for d in range(16):
                    dw_ref[pl.ds(c * 16 + d, WIDTH, stride=WIDTH), :] = fin_ref[c, d].astype(F32)
        outs[n].start()
    for copy in outs:
        copy.wait()


def shards(alignment, align_mask, residue_mask, left_weight, right_weight, out_weight, pair_cotangent):
    dma = pltpu.SemaphoreType.DMA
    vmem = pltpu.VMEM
    pair, ag, fin = pl.pallas_call(
        kernel,
        out_shape=(
            jax.ShapeDtypeStruct((RES, COLS, PAIR), BF16),
            jax.ShapeDtypeStruct((2 * RES, CH), BF16),
            jax.ShapeDtypeStruct((2, 16, WIDTH, PAIR), BF16),
        ),
        in_specs=[pl.BlockSpec(memory_space=pltpu.HBM)] * 7,
        out_specs=(pl.BlockSpec(memory_space=pl.ANY),) + (pl.BlockSpec(memory_space=pltpu.VMEM),) * 2,
        scratch_shapes=[
            vmem((2 * RES, CH), BF16), vmem((2, RES), jnp.int32), vmem((1, RES), jnp.int32),
            vmem((WIDTH, CH), BF16), vmem((WIDTH, CH), BF16), vmem((SIZE, PAIR), BF16),
            vmem((RES, COLS, PAIR), BF16), dma((7,)),
            vmem((16, 128), F32), vmem((4, 16, 128), BF16), vmem((16, 16, 128), BF16),
            vmem((4, 48, 128), BF16), vmem((2, 16, 48, 128), BF16), vmem((NSEQ, 48, 128), BF16),
            vmem((SIZE, PAIR), F32), vmem((WIDTH, WIDTH * PAIR), BF16), vmem((128, WIDTH * PAIR), BF16),
            vmem((RES * SEQS, 128), F32), vmem((RES * SEQS, 128), BF16),
            vmem((STEPS, WIDTH, BLOCK * SEQS), BF16), vmem((SIZE, SIZE), BF16),
            vmem((COLS, SIZE), BF16), vmem((COLS, 128), F32), vmem((COLS, SIZE), BF16),
            vmem((SIZE, COLS), BF16), vmem((COLS, 128), F32),
            vmem((STEPS, SIZE, BLOCK * PAIR), BF16), vmem((STEPS, BLOCK * SEQS, WIDTH * PAIR), BF16),
            vmem((STEPS, COLS, BLOCK * PAIR), BF16), vmem((SIZE, COLS), F32),
            vmem((RES * SEQS, 128), F32), vmem((WIDTH, WIDTH * PAIR), F32),
            vmem((RES, COLS, PAIR), BF16), dma((2,)),
            vmem((2, 16, 32, 128), BF16), vmem((16, 32, 128), BF16), vmem((16, 32, 128), BF16),
            vmem((16, 32, 128), BF16), vmem((16, 32, 128), BF16),
            vmem((2, 16, 32, 128), BF16), vmem((16, 32, 128), BF16), vmem((16, 32, 128), BF16),
            vmem((16, 32, 128), BF16), vmem((16, 16, 128), BF16), vmem((16, 16, 128), BF16),
            vmem((NSEQ, 32, 128), BF16), vmem((4, 4, 32, 128), BF16), vmem((4, 32, 128), BF16),
            vmem((4, 32, 128), BF16),
            dma((4, 2)), dma((4, 2)),
            dma((16,)), dma((16,)), dma((4,)), dma((4,)), dma((16,)), dma((16,)), dma((4,)), dma((4,)),
            dma((16,)), dma((16,)), dma((16,)), dma((16,)), dma((16,)), dma((16,)),
            dma((16,)), dma((16,)), dma((16,)), dma((16,)), dma((4,)), dma((4,)), dma((4,)), dma((4,)),
        ],
        compiler_params=pltpu.CompilerParams(
            collective_id=0, has_side_effects=True, vmem_limit_bytes=60000000
        ),
        name="pair_update",
    )(
        alignment.reshape(2 * RES, CH), align_mask, residue_mask.reshape(1, RES), left_weight.T, right_weight.T,
        out_weight, pair_cotangent.reshape(RES, COLS, PAIR),
    )
    anywhere = pl.BlockSpec(memory_space=pl.ANY)
    pair, ag, dw = pl.pallas_call(
        write_kernel,
        out_shape=(
            jax.ShapeDtypeStruct((RES, COLS, PAIR), BF16),
            jax.ShapeDtypeStruct((2 * RES, CH), BF16),
            jax.ShapeDtypeStruct((SIZE, PAIR), F32),
        ),
        in_specs=[anywhere] * 3,
        out_specs=(anywhere, anywhere, anywhere),
        scratch_shapes=[
            vmem((RES, COLS, PAIR), BF16), vmem((2 * RES, CH), BF16), vmem((2, 16, WIDTH, PAIR), BF16),
            vmem((SIZE, PAIR), F32), dma((10,)), dma((10,)),
        ],
        compiler_params=pltpu.CompilerParams(vmem_limit_bytes=60000000),
        name="write_outputs",
    )(pair, ag, fin)
    return pair.reshape(pair_cotangent.shape), ag.reshape(alignment.shape), dw


def solution(mesh):
    in_specs = (
        P("seq", "res", None),
        P("seq", "res"),
        P("res"),
        P(),
        P(),
        P(),
        P("res", None, "seq", None),
    )
    out_specs = (P("res", None, "seq", None), P("seq", "res", None), P())
    return jax.shard_map(shards, mesh=mesh, in_specs=in_specs, out_specs=out_specs, check_vma=False)
```

```python
import jax
import jax.numpy as jnp
from jax import lax
from jax.experimental import pallas as pl
from jax.experimental.pallas import tpu as pltpu
from jax.sharding import PartitionSpec as P

F32 = jnp.float32
BF16 = jnp.bfloat16
MESH = pl.DeviceIdType.MESH

NSEQ, SEQS, RES, WIDTH, CH, PAIR, COLS = 16, 32, 64, 32, 256, 128, 128
BLOCK = 8
STEPS = RES // BLOCK
EARLY = 4
SIZE = WIDTH * SEQS
NT_DIMS = (((1,), (1,)), ((), ()))


def iota(shape, dim):
    return lax.broadcasted_iota(jnp.int32, shape, dim)


def onehot(condition):
    return jnp.where(condition, 1.0, 0.0).astype(BF16)


def mm(a, b):
    return jnp.dot(a, b, preferred_element_type=F32)


def mm_nt(a, b):
    return lax.dot_general(a, b, NT_DIMS, preferred_element_type=F32)


def split(value):
    high = value.astype(BF16)
    return high, (value - high.astype(F32)).astype(BF16)


def as_column(row):
    n = row.shape[1]
    return jnp.sum(jnp.where(iota((n, n), 0) == iota((n, n), 1), row, 0.0), axis=1, keepdims=True)


def remote(src, dst, send, recv, device):
    return pltpu.make_async_remote_copy(
        src_ref=src, dst_ref=dst, send_sem=send, recv_sem=recv, device_id=device, device_id_type=MESH
    )


class Group:
    def __init__(self, count, me, device_of, source_of, slot_of, send, recv, peer_of=None):
        self.count, self.me, self.device_of = count, me, device_of
        self.peer_of = peer_of or (lambda k: (me + k) % count)
        self.source_of, self.slot_of, self.send, self.recv = source_of, slot_of, send, recv

    def each(self, body):
        if self.count <= 4:
            for k in (2, 1, 3) if self.count == 4 else (1,):
                body(k, self.peer_of(k))
        else:

            @pl.loop(0, self.count - 1)
            def _(k):
                body(k, self.peer_of(k))

    def out(self, k, other):
        return remote(
            self.source_of(other), self.slot_of(self.me), self.send.at[k], self.recv.at[self.me],
            self.device_of(other),
        )

    def start(self):
        self.each(lambda k, other: self.out(k, other).start())

    def wait(self):
        def body(k, other):
            slot = self.slot_of(other)
            remote(slot, slot, self.send.at[k], self.recv.at[other], self.device_of(other)).wait_recv()

        self.each(body)

    def sent(self):
        self.each(lambda k, other: self.out(k, other).wait_send())


def total(ref, first, count, span=slice(None)):
    value = ref[first, span].astype(F32)
    for n in range(1, count):
        value = value + ref[first + n, span].astype(F32)
    return value


def kernel(
    al_hbm, am_hbm, rm_hbm, wl_hbm, wr_hbm, w_hbm, ct_hbm,
    pair_hbm, ag_ref, fin,
    al_ref, am_ref, rm_ref, wl_ref, wr_ref, w_ref, ct_ref, in_sem,
    mask_ref, rsend, ra, rb, xr, lall,
    wf, wn, w4, lf, l2, lt, perm, rp, rm_all, rds, rt, rden, n_all, t_all, sc, rg, lgs, dw, pair_ref, pair_sem,
    wmsg, wcin, whalf, wxin, wz,
    rmsg, rcin, rhalf, rxin, rzs, rzin,
    lmsg, lx, lhalf, lz,
    c_send, c_recv,
    z_r_send, z_r_recv, z_l_send, z_l_recv, xy_r_send, xy_r_recv, x_l_send, x_l_recv,
    xy_w_send, xy_w_recv, z_w_send, z_w_recv, xy_f_send, xy_f_recv,
    xy_g_send, xy_g_recv, z_g_send, z_g_recv, x_g_send, x_g_recv, zl_g_send, zl_g_recv,
):
    a = lax.axis_index("seq")
    b = lax.axis_index("res")
    x, zh, core, y, zl = a // 4, a % 4, b % 2, b // 8, (b // 2) % 4
    xy, z = x * 4 + y, zh * 4 + zl
    z_device = lambda o: (x * 4 + o // 4, (y * 4 + o % 4) * 2 + core)
    xy_device = lambda o: ((o // 4) * 4 + zh, ((o % 4) * 4 + zl) * 2 + core)
    zh_device = lambda o: (x * 4 + o, b)
    x_device = lambda o: (o * 4 + zh, b)
    core_device = lambda o: (a, (y * 4 + zl) * 2 + o)

    def z_peer(k):
        return (z + 8 + ((k + 1) // 2) * (2 * (k % 2) - 1) + 16) % 16

    def turn(m):
        return 2 + (m * (m + 1)) // 2

    def xy_peer(k):
        return ((x + turn(k // 4)) % 4) * 4 + (y + turn(k % 4)) % 4

    def z_group(source_of, slot_of, send, recv):
        return Group(16, z, z_device, source_of, slot_of, send, recv, z_peer)

    def xy_group(source_of, slot_of, send, recv):
        return Group(16, xy, xy_device, source_of, slot_of, send, recv, xy_peer)

    def core_group(n, source_of, slot_of):
        return Group(2, core, core_device, source_of, slot_of, c_send.at[n], c_recv.at[n])

    loads = [
        pltpu.make_async_copy(src, dst, in_sem.at[n])
        for n, (src, dst) in enumerate(
            (
                (al_hbm, al_ref), (am_hbm, am_ref), (rm_hbm, rm_ref), (wl_hbm, wl_ref), (wr_hbm, wr_ref),
                (w_hbm, w_ref), (ct_hbm, ct_ref),
            )
        )
    ]
    barrier = pltpu.get_barrier_semaphore()

    @pl.loop(0, 15)
    def _(k):
        pl.semaphore_signal(barrier, inc=1, device_id=z_device(z_peer(k)), device_id_type=MESH)
        pl.semaphore_signal(barrier, inc=1, device_id=xy_device(xy_peer(k)), device_id_type=MESH)

    pl.semaphore_signal(barrier, inc=1, device_id=core_device(1 - core), device_id_type=MESH)
    for load in loads:
        load.start()
    for load in loads[:5]:
        load.wait()
    values = al_ref[...].astype(F32)
    center = values - jnp.mean(values, -1, keepdims=True)
    inverse = lax.rsqrt(jnp.mean(center * center, -1, keepdims=True) + 1e-05)
    rounded = (center * inverse).astype(BF16)
    w2 = (am_ref[...] * rm_ref[...]).astype(F32)
    row, lane = iota((128, WIDTH), 0), iota((128, WIDTH), 1)
    lanes = iota((RES, 128), 1)
    right = jnp.zeros((RES, 128), F32)
    left = jnp.zeros((32, 128), F32)
    for s in range(2):
        column = as_column(w2[s : s + 1])
        mine = rounded[s * RES : (s + 1) * RES]
        right_at = mm(onehot(row == lane + s * WIDTH), wr_ref[...]).astype(BF16)
        right = right + column * (mm_nt(mine, right_at) + jnp.where(lanes == 2 * WIDTH + s, 1.0, 0.0))
        for h in range(2):
            left_at = mm(onehot(row == lane + (2 * h + s) * WIDTH), wl_ref[...]).astype(BF16)
            span = slice(h * 32, (h + 1) * 32)
            left = left + column[span] * mm_nt(mine[span], left_at)
    r, col = iota((RES, RES), 0), iota((RES, RES), 1)
    order = onehot(col == ((r // 4) % 4) * 16 + (r // 16) * 4 + r % 4)
    right = mm(order, right.astype(BF16)).astype(BF16)
    for n in range(4):
        rsend[n] = right[n * 16 : (n + 1) * 16]
    mask_ref[...] = jnp.zeros((16, 128), F32)
    mask_ref[0:2, 0:RES] = w2
    lall[a, 0:32] = left.astype(BF16)
    lall[a, 32:48] = mask_ref[...].astype(BF16)
    loads[5].wait()
    wf[...] = w_ref[...].astype(F32)
    for d in range(WIDTH):
        piece = wf[pl.ds(d, WIDTH, stride=WIDTH), :].astype(BF16)
        wn[:, d * PAIR : (d + 1) * PAIR] = piece
        for q in range(4):
            w4[q * WIDTH : (q + 1) * WIDTH, d * PAIR : (d + 1) * PAIR] = piece
    pl.semaphore_wait(barrier, 31)
    z_r = z_group(lambda o: rsend.at[o // 4], lambda n: ra.at[n], z_r_send, z_r_recv)
    z_l = Group(
        4, zh, zh_device, lambda o: lall.at[a], lambda n: lall.at[x * 4 + n], z_l_send, z_l_recv
    )
    z_r.start()
    z_l.start()
    ra[z] = rsend[zh]
    for n in range(8):
        r, col = iota((SIZE // 8, SIZE), 0) + n * (SIZE // 8), iota((SIZE // 8, SIZE), 1)
        perm[n * (SIZE // 8) : (n + 1) * (SIZE // 8), :] = onehot(col == (r % 32) * 32 + r // 32)
    z_l.wait()
    x_l = Group(
        4, x, x_device, lambda o: lall.at[pl.ds(x * 4, 4)], lambda n: lall.at[pl.ds(n * 4, 4)],
        x_l_send, x_l_recv,
    )
    x_l.start()
    z_r.wait()

    r, col = iota((256, 256), 0), iota((256, 256), 1)
    order = onehot(col == ((r // 16) % 4) * 64 + ((r // 4) % 4) * 16 + (r // 64) * 4 + r % 4)
    moved = mm(order, ra[...].reshape(256, 128))
    lanes = iota((16, 128), 1)
    for n in range(4):
        part = [moved[n * 64 + h * 16 : n * 64 + (h + 1) * 16] for h in range(4)]
        masks = jnp.zeros((16, 128), F32)
        for h in range(4):
            own = jnp.where((lanes >= 64) & (lanes < 66), part[h], 0.0)
            masks = masks + pltpu.roll(own, (x * 8 + h * 2 + 64) % 128, 1)
        for t in range(2):
            tile = jnp.where(lanes < 64, part[2 * t], pltpu.roll(part[2 * t + 1], 64, 1))
            rb[n, t * 16 : (t + 1) * 16] = tile.astype(BF16)
        rb[n, 32:48] = masks.astype(BF16)
    xy_r = xy_group(lambda o: rb.at[o // 4], lambda n: xr.at[core, n], xy_r_send, xy_r_recv)
    xy_r.start()
    xr[core, xy] = rb[x]
    loads[6].wait()
    x_l.wait()
    blocks = lall[:, 0:32, :].reshape(NSEQ * 32, 128)
    row, lane = iota((128, 128), 0), iota((128, 128), 1)
    for h in range(2):
        for s in range(2):
            moved = mm(blocks, onehot((row == lane + (2 * h + s) * WIDTH) & (lane < WIDTH)))
            for n in range(NSEQ):
                lf[pl.ds(h * 32 * SEQS + 2 * n + s, 32, stride=SEQS), :] = moved[n * 32 : (n + 1) * 32]
    l2[...] = lf[...].astype(BF16)
    eye = onehot(iota((WIDTH, 128), 0) == iota((WIDTH, 128), 1))
    rows = BLOCK * SEQS
    for n in range(STEPS):
        lt[n] = mm_nt(eye, l2[n * rows : (n + 1) * rows, :]).astype(BF16)
    masks = lall[:, 32:48, :].astype(F32)[:, 0:8, :].reshape(128, 128).astype(BF16)
    r, col = iota((128, 128), 0), iota((128, 128), 1)
    left_mask = mm(onehot((r < SEQS) & (col == (r // 2) * 8 + r % 2)), masks).astype(BF16)
    xy_r.wait()
    c_r = core_group(0, lambda o: xr.at[core], lambda n: xr.at[n])
    c_r.start()
    def n_part(step):
        l2c = l2[step * rows : (step + 1) * rows, 0:WIDTH]
        for d2 in range(WIDTH // 2):
            part = mm(l2c, wn[:, d2 * 256 : (d2 + 1) * 256]).astype(BF16)
            for h in range(2):
                d = 2 * d2 + h
                for k in range(BLOCK):
                    n_all[step, d * SEQS : (d + 1) * SEQS, k * PAIR : (k + 1) * PAIR] = part[
                        k * SEQS : (k + 1) * SEQS, h * PAIR : (h + 1) * PAIR
                    ]

    for step in range(EARLY):
        n_part(step)
    c_r.wait()
    for c in range(2):
        for n in range(4):
            at = slice((c * 4 + n) * 16, (c * 4 + n + 1) * 16)
            rm_all[at] = sum(xr[c, m * 4 + n, 32:48].astype(F32) for m in range(4))
            for m in range(4):
                for t in range(2):
                    rp[at, m * 256 + t * 128 : m * 256 + (t + 1) * 128] = xr[
                        c, m * 4 + n, t * 16 : (t + 1) * 16
                    ]
    r, col = iota((128, 128), 0), iota((128, 128), 1)
    order = onehot(col == ((r // 4) % 2) * 64 + (r // 32) * 16 + ((r // 8) % 4) * 4 + r % 4)
    right_mask = mm(order, rm_all[...].astype(BF16)).astype(BF16)
    rden[...] = 1.0 / jnp.maximum(mm(right_mask, left_mask), 1.0)
    right = mm(order, rp[...]).astype(BF16)
    rds[...] = mm(right, perm[...]).astype(BF16)
    rt[...] = mm_nt(perm[...], right).astype(BF16)

    def scale_of(step):
        return pltpu.roll(rden[...], (128 - step * BLOCK) % 128, 1)
    dw[...] = jnp.zeros_like(dw)

    def t_part(step):
        scale = scale_of(step)
        for k in range(BLOCK):
            sc[step, :, k * PAIR : (k + 1) * PAIR] = (
                ct_ref[step * BLOCK + k].astype(F32) * scale[:, k : k + 1]
            ).astype(BF16)
        for k2 in range(BLOCK // 2):
            part = mm(rt[...], sc[step, :, k2 * 256 : (k2 + 1) * 256]).astype(BF16)
            for h in range(2):
                k = 2 * k2 + h
                for d in range(WIDTH):
                    t_all[step, k * SEQS : (k + 1) * SEQS, d * PAIR : (d + 1) * PAIR] = part[
                        d * SEQS : (d + 1) * SEQS, h * PAIR : (h + 1) * PAIR
                    ]

    for step in range(STEPS + 1):
        if step < STEPS:
            t_part(step)
        if step > 0:
            dw[...] += mm(lt[step - 1], t_all[step - 1])
    for c in range(2):
        for n in range(16):
            d = c * 16 + n
            wmsg[c, n] = dw[:, d * PAIR : (d + 1) * PAIR].astype(BF16)
    c_w = core_group(1, lambda o: wmsg.at[o], lambda n: wcin)
    c_w.start()
    rg[...] = jnp.zeros_like(rg)

    def right_part(step):
        rg[...] += mm_nt(n_all[step], sc[step])

    for step in range(EARLY):
        right_part(step)
    c_w.wait()
    for n in range(16):
        whalf[n] = (wmsg[core, n].astype(F32) + wcin[n].astype(F32)).astype(BF16)
    xy_w = xy_group(lambda o: whalf.at[o], lambda n: wxin.at[n], xy_w_send, xy_w_recv)
    xy_w.start()
    wxin[xy] = whalf[xy]
    for step in range(EARLY, STEPS):
        n_part(step)
    for step in range(EARLY, STEPS):
        right_part(step)
    r, col = iota((128, 128), 0), iota((128, 128), 1)
    order = onehot(col == ((r // 16) % 4) * 32 + ((r // 4) % 4) * 8 + (r // 64) * 4 + r % 4)
    grads = mm_nt(order, rg[...].astype(BF16)).astype(BF16)
    grads = mm(grads, perm[...]).astype(BF16)
    for c in range(2):
        for m in range(4):
            for n in range(4):
                at = slice((c * 4 + n) * 16, (c * 4 + n + 1) * 16)
                for t in range(2):
                    rmsg[c, m * 4 + n, t * 16 : (t + 1) * 16] = grads[
                        at, m * 256 + t * 128 : m * 256 + (t + 1) * 128
                    ]
    c_g = core_group(2, lambda o: rmsg.at[o], lambda n: rcin)
    c_g.start()
    def left_part(n):
        blocks = t_all[2 * n : 2 * n + 2].reshape(2 * rows, WIDTH * PAIR)
        lgs[n * 2 * rows : (n + 1) * 2 * rows, :] = mm_nt(blocks, w4[...])

    left_part(0)
    xy_w.wait()
    wz[z] = total(wxin, 0, 16).astype(BF16)
    z_w = z_group(lambda o: wz.at[z], lambda n: wz.at[n], z_w_send, z_w_recv)
    z_w.start()
    c_g.wait()
    for n in range(16):
        rhalf[n] = (rmsg[core, n].astype(F32) + rcin[n].astype(F32)).astype(BF16)
    xy_g = xy_group(lambda o: rhalf.at[o], lambda n: rxin.at[n], xy_g_send, xy_g_recv)
    xy_g.start()
    rxin[xy] = rhalf[xy]
    for n in range(1, STEPS // 2):
        left_part(n)
    lane = iota((32, 128), 1) // WIDTH
    for n in range(NSEQ):
        out = lgs[pl.ds(2 * n, 32, stride=SEQS), :]
        for q in range(1, 4):
            piece = lgs[pl.ds((q // 2) * 32 * SEQS + 2 * n + q % 2, 32, stride=SEQS), :]
            out = jnp.where(lane == q, piece, out)
        lmsg[n] = out.astype(BF16)
    x_g = Group(
        4, x, x_device, lambda o: lmsg.at[pl.ds(o * 4, 4)], lambda n: lx.at[n], x_g_send, x_g_recv
    )
    x_g.start()
    lx[x] = lmsg[pl.ds(x * 4, 4)]
    xy_g.wait()
    sums = [total(rxin, m * 4, 4).astype(BF16) for m in range(4)]
    r, col = iota((64, 64), 0), iota((64, 64), 1)
    order = onehot(col == ((r // 4) % 4) * 16 + (r // 16) * 4 + r % 4)
    for t in range(2):
        moved = mm(order, jnp.concatenate([v[t * 16 : (t + 1) * 16] for v in sums], axis=0))
        for h in range(2):
            own = moved if h == 0 else pltpu.roll(moved, 64, 1)
            for n in range(4):
                rzs[(2 * t + h) * 4 + n] = own[n * 16 : (n + 1) * 16].astype(BF16)
    z_g = z_group(lambda o: rzs.at[o], lambda n: rzin.at[n], z_g_send, z_g_recv)
    z_g.start()
    rzin[z] = rzs[z]
    z_w.wait()
    fin[core, xy] = total(wz, 0, 16).astype(BF16)
    xy_f = xy_group(lambda o: fin.at[core, xy], lambda n: fin.at[core, n], xy_f_send, xy_f_recv)
    xy_f.start()
    x_g.wait()
    lhalf[...] = total(lx, 0, 4).astype(BF16)
    zl_g = Group(4, zh, zh_device, lambda o: lhalf.at[o], lambda n: lz.at[n], zl_g_send, zl_g_recv)
    zl_g.start()
    lz[zh] = lhalf[zh]

    def pair_part(step):
        scale = scale_of(step)
        for k2 in range(BLOCK // 2):
            part = mm(rds[...], n_all[step, :, k2 * 256 : (k2 + 1) * 256])
            for h in range(2):
                k = 2 * k2 + h
                pair_ref[step * BLOCK + k] = (
                    part[:, h * PAIR : (h + 1) * PAIR] * scale[:, k : k + 1]
                ).astype(BF16)

    def pair_copy(n):
        span = pl.ds(n * (RES // 2), RES // 2)
        return pltpu.make_async_copy(pair_ref.at[span], pair_hbm.at[span], pair_sem.at[n])

    for step in range(STEPS):
        pair_part(step)
        if step == STEPS // 2 - 1:
            pair_copy(0).start()
    pair_copy(1).start()
    values = al_ref[...].astype(F32)
    center = values - jnp.mean(values, -1, keepdims=True)
    inverse = lax.rsqrt(jnp.mean(center * center, -1, keepdims=True) + 1e-05)
    normal = center * inverse
    w2 = (am_ref[...] * rm_ref[...]).astype(F32)
    right_at, left_at = [], []
    row, lane = iota((128, WIDTH), 0), iota((128, WIDTH), 1)
    for s in range(2):
        right_at.append(mm(onehot(row == lane + s * WIDTH), wr_ref[...]).astype(BF16))
        for h in range(2):
            left_at.append(mm(onehot(row == lane + (2 * h + s) * WIDTH), wl_ref[...]).astype(BF16))
    columns = [as_column(w2[s : s + 1]) for s in range(2)]
    for group in (z_r, z_l, xy_r, x_l, c_r, c_w, c_g, xy_w, z_w, xy_g, x_g):
        group.sent()
    xy_f.wait()
    c_f = core_group(3, lambda o: fin.at[core], lambda n: fin.at[n])
    c_f.start()
    zl_g.wait()
    left = split(total(lz, 0, 4))
    z_g.wait()
    r, col = iota((RES, RES), 0), iota((RES, RES), 1)
    order = onehot(col == ((r // 4) % 4) * 16 + (r // 16) * 4 + r % 4)
    right = split(jnp.concatenate([total(rzin, n * 4, 4) for n in range(4)], axis=0))
    right = [mm(order, v).astype(BF16) for v in right]
    for s in range(2):
        parts = [sum(mm(v, left_at[2 * s + h]) for v in left) for h in range(2)]
        grad = jnp.concatenate(parts, axis=0) + sum(mm(v, right_at[s]) for v in right)
        grad = grad * columns[s]
        span = slice(s * RES, (s + 1) * RES)
        first = jnp.mean(grad, -1, keepdims=True)
        second = jnp.mean(grad * normal[span], -1, keepdims=True)
        ag_ref[span] = (inverse[span] * (grad - first - normal[span] * second)).astype(BF16)
    for group in (xy_f, z_g, zl_g, c_f):
        group.sent()
    for n in range(2):
        pair_copy(n).wait()
    c_f.wait()


def write_kernel(pair_in, ag_in, fin_in, pair_out, ag_out, dw_out, pair_ref, ag_ref, fin_ref, dw_ref, sem, out_sem):
    count = 8
    rows = RES // count
    ins = [
        pltpu.make_async_copy(fin_in, fin_ref, sem.at[0]),
        pltpu.make_async_copy(ag_in, ag_ref, sem.at[1]),
    ]
    outs = [
        pltpu.make_async_copy(dw_ref, dw_out, out_sem.at[0]),
        pltpu.make_async_copy(ag_ref, ag_out, out_sem.at[1]),
    ]
    for n in range(count):
        span = pl.ds(n * rows, rows)
        ins.append(pltpu.make_async_copy(pair_in.at[span], pair_ref.at[span], sem.at[2 + n]))
        outs.append(pltpu.make_async_copy(pair_ref.at[span], pair_out.at[span], out_sem.at[2 + n]))
    for copy in ins:
        copy.start()
    for n, copy in enumerate(ins):
        copy.wait()
        if n == 0:
            for c in range(2):
                for d in range(16):
                    dw_ref[pl.ds(c * 16 + d, WIDTH, stride=WIDTH), :] = fin_ref[c, d].astype(F32)
        outs[n].start()
    for copy in outs:
        copy.wait()


def shards(alignment, align_mask, residue_mask, left_weight, right_weight, out_weight, pair_cotangent):
    dma = pltpu.SemaphoreType.DMA
    vmem = pltpu.VMEM
    pair, ag, fin = pl.pallas_call(
        kernel,
        out_shape=(
            jax.ShapeDtypeStruct((RES, COLS, PAIR), BF16),
            jax.ShapeDtypeStruct((2 * RES, CH), BF16),
            jax.ShapeDtypeStruct((2, 16, WIDTH, PAIR), BF16),
        ),
        in_specs=[pl.BlockSpec(memory_space=pltpu.HBM)] * 7,
        out_specs=(pl.BlockSpec(memory_space=pl.ANY),) + (pl.BlockSpec(memory_space=pltpu.VMEM),) * 2,
        scratch_shapes=[
            vmem((2 * RES, CH), BF16), vmem((2, RES), jnp.int32), vmem((1, RES), jnp.int32),
            vmem((WIDTH, CH), BF16), vmem((WIDTH, CH), BF16), vmem((SIZE, PAIR), BF16),
            vmem((RES, COLS, PAIR), BF16), dma((7,)),
            vmem((16, 128), F32), vmem((4, 16, 128), BF16), vmem((16, 16, 128), BF16),
            vmem((4, 48, 128), BF16), vmem((2, 16, 48, 128), BF16), vmem((NSEQ, 48, 128), BF16),
            vmem((SIZE, PAIR), F32), vmem((WIDTH, WIDTH * PAIR), BF16), vmem((128, WIDTH * PAIR), BF16),
            vmem((RES * SEQS, 128), F32), vmem((RES * SEQS, 128), BF16),
            vmem((STEPS, WIDTH, BLOCK * SEQS), BF16), vmem((SIZE, SIZE), BF16),
            vmem((COLS, SIZE), BF16), vmem((COLS, 128), F32), vmem((COLS, SIZE), BF16),
            vmem((SIZE, COLS), BF16), vmem((COLS, 128), F32),
            vmem((STEPS, SIZE, BLOCK * PAIR), BF16), vmem((STEPS, BLOCK * SEQS, WIDTH * PAIR), BF16),
            vmem((STEPS, COLS, BLOCK * PAIR), BF16), vmem((SIZE, COLS), F32),
            vmem((RES * SEQS, 128), F32), vmem((WIDTH, WIDTH * PAIR), F32),
            vmem((RES, COLS, PAIR), BF16), dma((2,)),
            vmem((2, 16, 32, 128), BF16), vmem((16, 32, 128), BF16), vmem((16, 32, 128), BF16),
            vmem((16, 32, 128), BF16), vmem((16, 32, 128), BF16),
            vmem((2, 16, 32, 128), BF16), vmem((16, 32, 128), BF16), vmem((16, 32, 128), BF16),
            vmem((16, 32, 128), BF16), vmem((16, 16, 128), BF16), vmem((16, 16, 128), BF16),
            vmem((NSEQ, 32, 128), BF16), vmem((4, 4, 32, 128), BF16), vmem((4, 32, 128), BF16),
            vmem((4, 32, 128), BF16),
            dma((4, 2)), dma((4, 2)),
            dma((16,)), dma((16,)), dma((4,)), dma((4,)), dma((16,)), dma((16,)), dma((4,)), dma((4,)),
            dma((16,)), dma((16,)), dma((16,)), dma((16,)), dma((16,)), dma((16,)),
            dma((16,)), dma((16,)), dma((16,)), dma((16,)), dma((4,)), dma((4,)), dma((4,)), dma((4,)),
        ],
        compiler_params=pltpu.CompilerParams(
            collective_id=0, has_side_effects=True, vmem_limit_bytes=60000000
        ),
        name="pair_update",
    )(
        alignment.reshape(2 * RES, CH), align_mask, residue_mask.reshape(1, RES), left_weight.T, right_weight.T,
        out_weight, pair_cotangent.reshape(RES, COLS, PAIR),
    )
    anywhere = pl.BlockSpec(memory_space=pl.ANY)
    pair, ag, dw = pl.pallas_call(
        write_kernel,
        out_shape=(
            jax.ShapeDtypeStruct((RES, COLS, PAIR), BF16),
            jax.ShapeDtypeStruct((2 * RES, CH), BF16),
            jax.ShapeDtypeStruct((SIZE, PAIR), F32),
        ),
        in_specs=[anywhere] * 3,
        out_specs=(anywhere, anywhere, anywhere),
        scratch_shapes=[
            vmem((RES, COLS, PAIR), BF16), vmem((2 * RES, CH), BF16), vmem((2, 16, WIDTH, PAIR), BF16),
            vmem((SIZE, PAIR), F32), dma((10,)), dma((10,)),
        ],
        compiler_params=pltpu.CompilerParams(vmem_limit_bytes=60000000),
        name="write_outputs",
    )(pair, ag, fin)
    return pair.reshape(pair_cotangent.shape), ag.reshape(alignment.shape), dw


def solution(mesh):
    in_specs = (
        P("seq", "res", None),
        P("seq", "res"),
        P("res"),
        P(),
        P(),
        P(),
        P("res", None, "seq", None),
    )
    out_specs = (P("res", None, "seq", None), P("seq", "res", None), P())
    return jax.shard_map(shards, mesh=mesh, in_specs=in_specs, out_specs=out_specs, check_vma=False)
```

```python
import jax
import jax.numpy as jnp
from jax import lax
from jax.experimental import pallas as pl
from jax.experimental.pallas import tpu as pltpu
from jax.sharding import PartitionSpec as P

F32 = jnp.float32
BF16 = jnp.bfloat16
MESH = pl.DeviceIdType.MESH

NSEQ, SEQS, RES, WIDTH, CH, PAIR, COLS = 16, 32, 64, 32, 256, 128, 128
BLOCK = 8
STEPS = RES // BLOCK
EARLY = 4
SIZE = WIDTH * SEQS
NT_DIMS = (((1,), (1,)), ((), ()))


def iota(shape, dim):
    return lax.broadcasted_iota(jnp.int32, shape, dim)


def onehot(condition):
    return jnp.where(condition, 1.0, 0.0).astype(BF16)


def mm(a, b):
    return jnp.dot(a, b, preferred_element_type=F32)


def mm_nt(a, b):
    return lax.dot_general(a, b, NT_DIMS, preferred_element_type=F32)


def split(value):
    high = value.astype(BF16)
    return high, (value - high.astype(F32)).astype(BF16)


def as_column(row):
    n = row.shape[1]
    return jnp.sum(jnp.where(iota((n, n), 0) == iota((n, n), 1), row, 0.0), axis=1, keepdims=True)


def remote(src, dst, send, recv, device):
    return pltpu.make_async_remote_copy(
        src_ref=src, dst_ref=dst, send_sem=send, recv_sem=recv, device_id=device, device_id_type=MESH
    )


class Group:
    def __init__(self, count, me, device_of, source_of, slot_of, send, recv, peer_of=None):
        self.count, self.me, self.device_of = count, me, device_of
        self.peer_of = peer_of or (lambda k: (me + k) % count)
        self.source_of, self.slot_of, self.send, self.recv = source_of, slot_of, send, recv

    def each(self, body):
        if self.count <= 4:
            for k in (2, 1, 3) if self.count == 4 else (1,):
                body(k, self.peer_of(k))
        else:

            @pl.loop(0, self.count - 1)
            def _(k):
                body(k, self.peer_of(k))

    def out(self, k, other):
        return remote(
            self.source_of(other), self.slot_of(self.me), self.send.at[k], self.recv.at[self.me],
            self.device_of(other),
        )

    def start(self):
        self.each(lambda k, other: self.out(k, other).start())

    def wait(self):
        def body(k, other):
            slot = self.slot_of(other)
            remote(slot, slot, self.send.at[k], self.recv.at[other], self.device_of(other)).wait_recv()

        self.each(body)

    def sent(self):
        self.each(lambda k, other: self.out(k, other).wait_send())


def total(ref, first, count, span=slice(None)):
    value = ref[first, span].astype(F32)
    for n in range(1, count):
        value = value + ref[first + n, span].astype(F32)
    return value


def kernel(
    al_hbm, am_hbm, rm_hbm, wl_hbm, wr_hbm, w_hbm, ct_hbm,
    pair_hbm, ag_hbm, fin_hbm,
    al_ref, am_ref, rm_ref, wl_ref, wr_ref, w_ref, ct_ref, in_sem,
    mask_ref, rsend, ra, rb, xr, lall,
    wf, wn, w4, lf, l2, lt, perm, rp, rm_all, rds, rt, rden, n_all, t_all, sc, rg, lgs, dw, pair_ref, ag_ref, fin, out_sem,
    wmsg, wcin, whalf, wxin, wz,
    rmsg, rcin, rhalf, rxin, rzs, rzin,
    lmsg, lx, lhalf, lz,
    c_send, c_recv,
    z_r_send, z_r_recv, z_l_send, z_l_recv, xy_r_send, xy_r_recv, x_l_send, x_l_recv,
    xy_w_send, xy_w_recv, z_w_send, z_w_recv, xy_f_send, xy_f_recv,
    xy_g_send, xy_g_recv, z_g_send, z_g_recv, x_g_send, x_g_recv, zl_g_send, zl_g_recv,
):
    a = lax.axis_index("seq")
    b = lax.axis_index("res")
    x, zh, core, y, zl = a // 4, a % 4, b % 2, b // 8, (b // 2) % 4
    xy, z = x * 4 + y, zh * 4 + zl
    z_device = lambda o: (x * 4 + o // 4, (y * 4 + o % 4) * 2 + core)
    xy_device = lambda o: ((o // 4) * 4 + zh, ((o % 4) * 4 + zl) * 2 + core)
    zh_device = lambda o: (x * 4 + o, b)
    x_device = lambda o: (o * 4 + zh, b)
    core_device = lambda o: (a, (y * 4 + zl) * 2 + o)

    def z_peer(k):
        return (z + 8 + ((k + 1) // 2) * (2 * (k % 2) - 1) + 16) % 16

    def turn(m):
        return 2 + (m * (m + 1)) // 2

    def xy_peer(k):
        return ((x + turn(k // 4)) % 4) * 4 + (y + turn(k % 4)) % 4

    def z_group(source_of, slot_of, send, recv):
        return Group(16, z, z_device, source_of, slot_of, send, recv, z_peer)

    def xy_group(source_of, slot_of, send, recv):
        return Group(16, xy, xy_device, source_of, slot_of, send, recv, xy_peer)

    def core_group(n, source_of, slot_of):
        return Group(2, core, core_device, source_of, slot_of, c_send.at[n], c_recv.at[n])

    loads = [
        pltpu.make_async_copy(src, dst, in_sem.at[n])
        for n, (src, dst) in enumerate(
            (
                (al_hbm, al_ref), (am_hbm, am_ref), (rm_hbm, rm_ref), (wl_hbm, wl_ref), (wr_hbm, wr_ref),
                (w_hbm, w_ref), (ct_hbm, ct_ref),
            )
        )
    ]
    barrier = pltpu.get_barrier_semaphore()

    @pl.loop(0, 15)
    def _(k):
        pl.semaphore_signal(barrier, inc=1, device_id=z_device(z_peer(k)), device_id_type=MESH)
        pl.semaphore_signal(barrier, inc=1, device_id=xy_device(xy_peer(k)), device_id_type=MESH)

    pl.semaphore_signal(barrier, inc=1, device_id=core_device(1 - core), device_id_type=MESH)
    for load in loads:
        load.start()
    for load in loads[:5]:
        load.wait()
    values = al_ref[...].astype(F32)
    center = values - jnp.mean(values, -1, keepdims=True)
    inverse = lax.rsqrt(jnp.mean(center * center, -1, keepdims=True) + 1e-05)
    rounded = (center * inverse).astype(BF16)
    w2 = (am_ref[...] * rm_ref[...]).astype(F32)
    row, lane = iota((128, WIDTH), 0), iota((128, WIDTH), 1)
    lanes = iota((RES, 128), 1)
    right = jnp.zeros((RES, 128), F32)
    left = jnp.zeros((32, 128), F32)
    for s in range(2):
        column = as_column(w2[s : s + 1])
        mine = rounded[s * RES : (s + 1) * RES]
        right_at = mm(onehot(row == lane + s * WIDTH), wr_ref[...]).astype(BF16)
        right = right + column * (mm_nt(mine, right_at) + jnp.where(lanes == 2 * WIDTH + s, 1.0, 0.0))
        for h in range(2):
            left_at = mm(onehot(row == lane + (2 * h + s) * WIDTH), wl_ref[...]).astype(BF16)
            span = slice(h * 32, (h + 1) * 32)
            left = left + column[span] * mm_nt(mine[span], left_at)
    r, col = iota((RES, RES), 0), iota((RES, RES), 1)
    order = onehot(col == ((r // 4) % 4) * 16 + (r // 16) * 4 + r % 4)
    right = mm(order, right.astype(BF16)).astype(BF16)
    for n in range(4):
        rsend[n] = right[n * 16 : (n + 1) * 16]
    mask_ref[...] = jnp.zeros((16, 128), F32)
    mask_ref[0:2, 0:RES] = w2
    lall[a, 0:32] = left.astype(BF16)
    lall[a, 32:48] = mask_ref[...].astype(BF16)
    loads[5].wait()
    wf[...] = w_ref[...].astype(F32)
    for d in range(WIDTH):
        piece = wf[pl.ds(d, WIDTH, stride=WIDTH), :].astype(BF16)
        wn[:, d * PAIR : (d + 1) * PAIR] = piece
        for q in range(4):
            w4[q * WIDTH : (q + 1) * WIDTH, d * PAIR : (d + 1) * PAIR] = piece
    pl.semaphore_wait(barrier, 31)
    z_r = z_group(lambda o: rsend.at[o // 4], lambda n: ra.at[n], z_r_send, z_r_recv)
    z_l = Group(
        4, zh, zh_device, lambda o: lall.at[a], lambda n: lall.at[x * 4 + n], z_l_send, z_l_recv
    )
    z_r.start()
    z_l.start()
    ra[z] = rsend[zh]
    for n in range(8):
        r, col = iota((SIZE // 8, SIZE), 0) + n * (SIZE // 8), iota((SIZE // 8, SIZE), 1)
        perm[n * (SIZE // 8) : (n + 1) * (SIZE // 8), :] = onehot(col == (r % 32) * 32 + r // 32)
    z_l.wait()
    x_l = Group(
        4, x, x_device, lambda o: lall.at[pl.ds(x * 4, 4)], lambda n: lall.at[pl.ds(n * 4, 4)],
        x_l_send, x_l_recv,
    )
    x_l.start()
    z_r.wait()

    r, col = iota((256, 256), 0), iota((256, 256), 1)
    order = onehot(col == ((r // 16) % 4) * 64 + ((r // 4) % 4) * 16 + (r // 64) * 4 + r % 4)
    moved = mm(order, ra[...].reshape(256, 128))
    lanes = iota((16, 128), 1)
    for n in range(4):
        part = [moved[n * 64 + h * 16 : n * 64 + (h + 1) * 16] for h in range(4)]
        masks = jnp.zeros((16, 128), F32)
        for h in range(4):
            own = jnp.where((lanes >= 64) & (lanes < 66), part[h], 0.0)
            masks = masks + pltpu.roll(own, (x * 8 + h * 2 + 64) % 128, 1)
        for t in range(2):
            tile = jnp.where(lanes < 64, part[2 * t], pltpu.roll(part[2 * t + 1], 64, 1))
            rb[n, t * 16 : (t + 1) * 16] = tile.astype(BF16)
        rb[n, 32:48] = masks.astype(BF16)
    xy_r = xy_group(lambda o: rb.at[o // 4], lambda n: xr.at[core, n], xy_r_send, xy_r_recv)
    xy_r.start()
    xr[core, xy] = rb[x]
    loads[6].wait()
    x_l.wait()
    blocks = lall[:, 0:32, :].reshape(NSEQ * 32, 128)
    row, lane = iota((128, 128), 0), iota((128, 128), 1)
    for h in range(2):
        for s in range(2):
            moved = mm(blocks, onehot((row == lane + (2 * h + s) * WIDTH) & (lane < WIDTH)))
            for n in range(NSEQ):
                lf[pl.ds(h * 32 * SEQS + 2 * n + s, 32, stride=SEQS), :] = moved[n * 32 : (n + 1) * 32]
    l2[...] = lf[...].astype(BF16)
    eye = onehot(iota((WIDTH, 128), 0) == iota((WIDTH, 128), 1))
    rows = BLOCK * SEQS
    for n in range(STEPS):
        lt[n] = mm_nt(eye, l2[n * rows : (n + 1) * rows, :]).astype(BF16)
    masks = lall[:, 32:48, :].astype(F32)[:, 0:8, :].reshape(128, 128).astype(BF16)
    r, col = iota((128, 128), 0), iota((128, 128), 1)
    left_mask = mm(onehot((r < SEQS) & (col == (r // 2) * 8 + r % 2)), masks).astype(BF16)
    xy_r.wait()
    c_r = core_group(0, lambda o: xr.at[core], lambda n: xr.at[n])
    c_r.start()
    def n_part(step):
        l2c = l2[step * rows : (step + 1) * rows, 0:WIDTH]
        for d2 in range(WIDTH // 2):
            part = mm(l2c, wn[:, d2 * 256 : (d2 + 1) * 256]).astype(BF16)
            for h in range(2):
                d = 2 * d2 + h
                for k in range(BLOCK):
                    n_all[step, d * SEQS : (d + 1) * SEQS, k * PAIR : (k + 1) * PAIR] = part[
                        k * SEQS : (k + 1) * SEQS, h * PAIR : (h + 1) * PAIR
                    ]

    for step in range(EARLY):
        n_part(step)
    c_r.wait()
    for c in range(2):
        for n in range(4):
            at = slice((c * 4 + n) * 16, (c * 4 + n + 1) * 16)
            rm_all[at] = sum(xr[c, m * 4 + n, 32:48].astype(F32) for m in range(4))
            for m in range(4):
                for t in range(2):
                    rp[at, m * 256 + t * 128 : m * 256 + (t + 1) * 128] = xr[
                        c, m * 4 + n, t * 16 : (t + 1) * 16
                    ]
    r, col = iota((128, 128), 0), iota((128, 128), 1)
    order = onehot(col == ((r // 4) % 2) * 64 + (r // 32) * 16 + ((r // 8) % 4) * 4 + r % 4)
    right_mask = mm(order, rm_all[...].astype(BF16)).astype(BF16)
    rden[...] = 1.0 / jnp.maximum(mm(right_mask, left_mask), 1.0)
    right = mm(order, rp[...]).astype(BF16)
    rp[...] = right
    rt[...] = mm_nt(perm[...], right).astype(BF16)

    def scale_of(step):
        return pltpu.roll(rden[...], (128 - step * BLOCK) % 128, 1)
    dw[...] = jnp.zeros_like(dw)

    def t_part(step):
        scale = scale_of(step)
        for k in range(BLOCK):
            sc[step, :, k * PAIR : (k + 1) * PAIR] = (
                ct_ref[step * BLOCK + k].astype(F32) * scale[:, k : k + 1]
            ).astype(BF16)
        for k2 in range(BLOCK // 2):
            part = mm(rt[...], sc[step, :, k2 * 256 : (k2 + 1) * 256]).astype(BF16)
            for h in range(2):
                k = 2 * k2 + h
                for d in range(WIDTH):
                    t_all[step, k * SEQS : (k + 1) * SEQS, d * PAIR : (d + 1) * PAIR] = part[
                        d * SEQS : (d + 1) * SEQS, h * PAIR : (h + 1) * PAIR
                    ]

    for step in range(STEPS + 1):
        if step < STEPS:
            t_part(step)
        if step > 0:
            dw[...] += mm(lt[step - 1], t_all[step - 1])
    for c in range(2):
        for n in range(16):
            d = c * 16 + n
            wmsg[c, n] = dw[:, d * PAIR : (d + 1) * PAIR].astype(BF16)
    c_w = core_group(1, lambda o: wmsg.at[o], lambda n: wcin)
    c_w.start()
    rg[...] = jnp.zeros_like(rg)

    def right_part(step):
        rg[...] += mm_nt(n_all[step], sc[step])

    for step in range(EARLY):
        right_part(step)
    c_w.wait()
    for n in range(16):
        whalf[n] = (wmsg[core, n].astype(F32) + wcin[n].astype(F32)).astype(BF16)
    xy_w = xy_group(lambda o: whalf.at[o], lambda n: wxin.at[n], xy_w_send, xy_w_recv)
    xy_w.start()
    wxin[xy] = whalf[xy]
    for step in range(EARLY, STEPS):
        n_part(step)
    for step in range(EARLY, STEPS):
        right_part(step)
    r, col = iota((128, 128), 0), iota((128, 128), 1)
    order = onehot(col == ((r // 16) % 4) * 32 + ((r // 4) % 4) * 8 + (r // 64) * 4 + r % 4)
    grads = mm_nt(order, rg[...].astype(BF16)).astype(BF16)
    grads = mm(grads, perm[...]).astype(BF16)
    for c in range(2):
        for m in range(4):
            for n in range(4):
                at = slice((c * 4 + n) * 16, (c * 4 + n + 1) * 16)
                for t in range(2):
                    rmsg[c, m * 4 + n, t * 16 : (t + 1) * 16] = grads[
                        at, m * 256 + t * 128 : m * 256 + (t + 1) * 128
                    ]
    c_g = core_group(2, lambda o: rmsg.at[o], lambda n: rcin)
    c_g.start()
    def left_part(n):
        blocks = t_all[2 * n : 2 * n + 2].reshape(2 * rows, WIDTH * PAIR)
        lgs[n * 2 * rows : (n + 1) * 2 * rows, :] = mm_nt(blocks, w4[...])

    left_part(0)
    xy_w.wait()
    wz[z] = total(wxin, 0, 16).astype(BF16)
    z_w = z_group(lambda o: wz.at[z], lambda n: wz.at[n], z_w_send, z_w_recv)
    z_w.start()
    c_g.wait()
    for n in range(16):
        rhalf[n] = (rmsg[core, n].astype(F32) + rcin[n].astype(F32)).astype(BF16)
    xy_g = xy_group(lambda o: rhalf.at[o], lambda n: rxin.at[n], xy_g_send, xy_g_recv)
    xy_g.start()
    rxin[xy] = rhalf[xy]
    for n in range(1, STEPS // 2):
        left_part(n)
    lane = iota((32, 128), 1) // WIDTH
    for n in range(NSEQ):
        out = lgs[pl.ds(2 * n, 32, stride=SEQS), :]
        for q in range(1, 4):
            piece = lgs[pl.ds((q // 2) * 32 * SEQS + 2 * n + q % 2, 32, stride=SEQS), :]
            out = jnp.where(lane == q, piece, out)
        lmsg[n] = out.astype(BF16)
    x_g = Group(
        4, x, x_device, lambda o: lmsg.at[pl.ds(o * 4, 4)], lambda n: lx.at[n], x_g_send, x_g_recv
    )
    x_g.start()
    lx[x] = lmsg[pl.ds(x * 4, 4)]
    xy_g.wait()
    sums = [total(rxin, m * 4, 4).astype(BF16) for m in range(4)]
    r, col = iota((64, 64), 0), iota((64, 64), 1)
    order = onehot(col == ((r // 4) % 4) * 16 + (r // 16) * 4 + r % 4)
    for t in range(2):
        moved = mm(order, jnp.concatenate([v[t * 16 : (t + 1) * 16] for v in sums], axis=0))
        for h in range(2):
            own = moved if h == 0 else pltpu.roll(moved, 64, 1)
            for n in range(4):
                rzs[(2 * t + h) * 4 + n] = own[n * 16 : (n + 1) * 16].astype(BF16)
    z_g = z_group(lambda o: rzs.at[o], lambda n: rzin.at[n], z_g_send, z_g_recv)
    z_g.start()
    rzin[z] = rzs[z]
    z_w.wait()
    fin[core, xy] = total(wz, 0, 16).astype(BF16)
    xy_f = xy_group(lambda o: fin.at[core, xy], lambda n: fin.at[core, n], xy_f_send, xy_f_recv)
    xy_f.start()
    x_g.wait()
    lhalf[...] = total(lx, 0, 4).astype(BF16)
    zl_g = Group(4, zh, zh_device, lambda o: lhalf.at[o], lambda n: lz.at[n], zl_g_send, zl_g_recv)
    zl_g.start()
    lz[zh] = lhalf[zh]

    rds[...] = mm(rp[...], perm[...]).astype(BF16)

    def pair_part(step):
        scale = scale_of(step)
        for k2 in range(BLOCK // 2):
            part = mm(rds[...], n_all[step, :, k2 * 256 : (k2 + 1) * 256])
            for h in range(2):
                k = 2 * k2 + h
                pair_ref[step * BLOCK + k] = (
                    part[:, h * PAIR : (h + 1) * PAIR] * scale[:, k : k + 1]
                ).astype(BF16)

    def pair_copy(n):
        span = pl.ds(n * (RES // 2), RES // 2)
        return pltpu.make_async_copy(pair_ref.at[span], pair_hbm.at[span], out_sem.at[n])

    for step in range(STEPS):
        pair_part(step)
        if step == STEPS // 2 - 1:
            pair_copy(0).start()
    pair_copy(1).start()
    values = al_ref[...].astype(F32)
    center = values - jnp.mean(values, -1, keepdims=True)
    inverse = lax.rsqrt(jnp.mean(center * center, -1, keepdims=True) + 1e-05)
    normal = center * inverse
    w2 = (am_ref[...] * rm_ref[...]).astype(F32)
    right_at, left_at = [], []
    row, lane = iota((128, WIDTH), 0), iota((128, WIDTH), 1)
    for s in range(2):
        right_at.append(mm(onehot(row == lane + s * WIDTH), wr_ref[...]).astype(BF16))
        for h in range(2):
            left_at.append(mm(onehot(row == lane + (2 * h + s) * WIDTH), wl_ref[...]).astype(BF16))
    columns = [as_column(w2[s : s + 1]) for s in range(2)]
    for group in (z_r, z_l, xy_r, x_l, c_r, c_w, c_g, xy_w, z_w, xy_g, x_g):
        group.sent()
    xy_f.wait()
    c_f = core_group(3, lambda o: fin.at[core], lambda n: fin_hbm.at[n])
    c_f.start()
    fin_copy = pltpu.make_async_copy(fin.at[core], fin_hbm.at[core], out_sem.at[2])
    fin_copy.start()
    zl_g.wait()
    left = split(total(lz, 0, 4))
    z_g.wait()
    r, col = iota((RES, RES), 0), iota((RES, RES), 1)
    order = onehot(col == ((r // 4) % 4) * 16 + (r // 16) * 4 + r % 4)
    right = split(jnp.concatenate([total(rzin, n * 4, 4) for n in range(4)], axis=0))
    right = [mm(order, v).astype(BF16) for v in right]
    for s in range(2):
        parts = [sum(mm(v, left_at[2 * s + h]) for v in left) for h in range(2)]
        grad = jnp.concatenate(parts, axis=0) + sum(mm(v, right_at[s]) for v in right)
        grad = grad * columns[s]
        span = slice(s * RES, (s + 1) * RES)
        first = jnp.mean(grad, -1, keepdims=True)
        second = jnp.mean(grad * normal[span], -1, keepdims=True)
        ag_ref[span] = (inverse[span] * (grad - first - normal[span] * second)).astype(BF16)
    ag_copy = pltpu.make_async_copy(ag_ref, ag_hbm, out_sem.at[3])
    ag_copy.start()
    for group in (xy_f, z_g, zl_g, c_f):
        group.sent()
    fin_copy.wait()
    ag_copy.wait()
    for n in range(2):
        pair_copy(n).wait()
    c_f.wait()


def write_kernel(pair_in, ag_in, fin_in, pair_out, ag_out, dw_out, pair_ref, ag_ref, fin_ref, dw_ref, sem, out_sem):
    count = 8
    rows = RES // count
    ins = [
        pltpu.make_async_copy(fin_in, fin_ref, sem.at[0]),
        pltpu.make_async_copy(ag_in, ag_ref, sem.at[1]),
    ]
    outs = [
        pltpu.make_async_copy(dw_ref, dw_out, out_sem.at[0]),
        pltpu.make_async_copy(ag_ref, ag_out, out_sem.at[1]),
    ]
    for n in range(count):
        span = pl.ds(n * rows, rows)
        ins.append(pltpu.make_async_copy(pair_in.at[span], pair_ref.at[span], sem.at[2 + n]))
        outs.append(pltpu.make_async_copy(pair_ref.at[span], pair_out.at[span], out_sem.at[2 + n]))
    for copy in ins:
        copy.start()
    for n, copy in enumerate(ins):
        copy.wait()
        if n == 0:
            for c in range(2):
                for d in range(16):
                    dw_ref[pl.ds(c * 16 + d, WIDTH, stride=WIDTH), :] = fin_ref[c, d].astype(F32)
        outs[n].start()
    for copy in outs:
        copy.wait()


def shards(alignment, align_mask, residue_mask, left_weight, right_weight, out_weight, pair_cotangent):
    dma = pltpu.SemaphoreType.DMA
    vmem = pltpu.VMEM
    pair, ag, fin = pl.pallas_call(
        kernel,
        out_shape=(
            jax.ShapeDtypeStruct((RES, COLS, PAIR), BF16),
            jax.ShapeDtypeStruct((2 * RES, CH), BF16),
            jax.ShapeDtypeStruct((2, 16, WIDTH, PAIR), BF16),
        ),
        in_specs=[pl.BlockSpec(memory_space=pltpu.HBM)] * 7,
        out_specs=(pl.BlockSpec(memory_space=pl.ANY),) * 3,
        scratch_shapes=[
            vmem((2 * RES, CH), BF16), vmem((2, RES), jnp.int32), vmem((1, RES), jnp.int32),
            vmem((WIDTH, CH), BF16), vmem((WIDTH, CH), BF16), vmem((SIZE, PAIR), BF16),
            vmem((RES, COLS, PAIR), BF16), dma((7,)),
            vmem((16, 128), F32), vmem((4, 16, 128), BF16), vmem((16, 16, 128), BF16),
            vmem((4, 48, 128), BF16), vmem((2, 16, 48, 128), BF16), vmem((NSEQ, 48, 128), BF16),
            vmem((SIZE, PAIR), F32), vmem((WIDTH, WIDTH * PAIR), BF16), vmem((128, WIDTH * PAIR), BF16),
            vmem((RES * SEQS, 128), F32), vmem((RES * SEQS, 128), BF16),
            vmem((STEPS, WIDTH, BLOCK * SEQS), BF16), vmem((SIZE, SIZE), BF16),
            vmem((COLS, SIZE), BF16), vmem((COLS, 128), F32), vmem((COLS, SIZE), BF16),
            vmem((SIZE, COLS), BF16), vmem((COLS, 128), F32),
            vmem((STEPS, SIZE, BLOCK * PAIR), BF16), vmem((STEPS, BLOCK * SEQS, WIDTH * PAIR), BF16),
            vmem((STEPS, COLS, BLOCK * PAIR), BF16), vmem((SIZE, COLS), F32),
            vmem((RES * SEQS, 128), F32), vmem((WIDTH, WIDTH * PAIR), F32),
            vmem((RES, COLS, PAIR), BF16), vmem((2 * RES, CH), BF16), vmem((2, 16, WIDTH, PAIR), BF16), dma((4,)),
            vmem((2, 16, 32, 128), BF16), vmem((16, 32, 128), BF16), vmem((16, 32, 128), BF16),
            vmem((16, 32, 128), BF16), vmem((16, 32, 128), BF16),
            vmem((2, 16, 32, 128), BF16), vmem((16, 32, 128), BF16), vmem((16, 32, 128), BF16),
            vmem((16, 32, 128), BF16), vmem((16, 16, 128), BF16), vmem((16, 16, 128), BF16),
            vmem((NSEQ, 32, 128), BF16), vmem((4, 4, 32, 128), BF16), vmem((4, 32, 128), BF16),
            vmem((4, 32, 128), BF16),
            dma((4, 2)), dma((4, 2)),
            dma((16,)), dma((16,)), dma((4,)), dma((4,)), dma((16,)), dma((16,)), dma((4,)), dma((4,)),
            dma((16,)), dma((16,)), dma((16,)), dma((16,)), dma((16,)), dma((16,)),
            dma((16,)), dma((16,)), dma((16,)), dma((16,)), dma((4,)), dma((4,)), dma((4,)), dma((4,)),
        ],
        compiler_params=pltpu.CompilerParams(
            collective_id=0, has_side_effects=True, vmem_limit_bytes=60000000
        ),
        name="pair_update",
    )(
        alignment.reshape(2 * RES, CH), align_mask, residue_mask.reshape(1, RES), left_weight.T, right_weight.T,
        out_weight, pair_cotangent.reshape(RES, COLS, PAIR),
    )
    anywhere = pl.BlockSpec(memory_space=pl.ANY)
    pair, ag, dw = pl.pallas_call(
        write_kernel,
        out_shape=(
            jax.ShapeDtypeStruct((RES, COLS, PAIR), BF16),
            jax.ShapeDtypeStruct((2 * RES, CH), BF16),
            jax.ShapeDtypeStruct((SIZE, PAIR), F32),
        ),
        in_specs=[anywhere] * 3,
        out_specs=(anywhere, anywhere, anywhere),
        scratch_shapes=[
            vmem((RES, COLS, PAIR), BF16), vmem((2 * RES, CH), BF16), vmem((2, 16, WIDTH, PAIR), BF16),
            vmem((SIZE, PAIR), F32), dma((10,)), dma((10,)),
        ],
        compiler_params=pltpu.CompilerParams(vmem_limit_bytes=60000000),
        name="write_outputs",
    )(pair, ag, fin)
    return pair.reshape(pair_cotangent.shape), ag.reshape(alignment.shape), dw


def solution(mesh):
    in_specs = (
        P("seq", "res", None),
        P("seq", "res"),
        P("res"),
        P(),
        P(),
        P(),
        P("res", None, "seq", None),
    )
    out_specs = (P("res", None, "seq", None), P("seq", "res", None), P())
    return jax.shard_map(shards, mesh=mesh, in_specs=in_specs, out_specs=out_specs, check_vma=False)
```
